256 devices in a mesh: ctx: 8 (over z), head: 4 (over x_hi, core), row: 8 (over x_lo, y).
Axes of the slice: x: 4 (x_hi: 2, x_lo: 2; x = x_hi * 2 + x_lo), y: 4, z: 8, core: 2. Of those that a mesh axis runs over, the one named last changes fastest.
Arguments:
- hidden: bfloat16 [3072, 8192], P(('ctx', 'row')), may hold values from -6 to 6
- norm_gain: bfloat16 [8192], replicated, may hold values from 0.099609375 to 1.8984375
- q_weight: bfloat16 [8192, 4096], P(None, ('head', 'row')), may hold values from -0.09375 to 0.09375
- q_bias: bfloat16 [4096], P(('head', 'row')), may hold values from -3 to 3
- key_weight: bfloat16 [8192, 512], P(None, 'head'), may hold values from -0.0625 to 0.0625
- key_bias: bfloat16 [512], P('head'), may hold values from -3 to 3
- value_weight: bfloat16 [8192, 512], P(None, 'head'), may hold values from -0.0625 to 0.0625
- value_bias: bfloat16 [512], P('head'), may hold values from -3 to 3
- o_weight: bfloat16 [4096, 8192], P(('head', 'row')), may hold values from -6 to 6
- cached_key_rows: bfloat16 [32768, 512], P('ctx', 'head'), may hold values from -256 to 256
- cached_value_rows: bfloat16 [32768, 512], P('ctx', 'head'), may hold values from -6 to 6
- keep_blocks: int32 [8, 8], P('ctx'), may hold values from 0 to 31, as said below
- kept_counts: int32 [8], replicated, may hold values from 2 to 8, as said below
- span_start: int32 [1], replicated, may hold values from 32768 to 36863
Outputs:
- output: bfloat16 [3072, 8192], P('ctx', ('head', 'row'))
The draws below stay inside these ranges and needn't reach their ends.
Inputs may be any that keep to these rules, and one draw needn't show every extreme that they name: `keep_blocks`: row g lists in increasing order the kept_counts[g] distinct kept blocks among group g's 32 prefix blocks; its remaining entries are 0. `kept_counts`: one group keeps 8 blocks and another keeps 8 // 4.
All inputs are finite; a program needn't handle non-finite values.
Results may differ from the reference program's by a relative error of at most 0.014.
Values may be sent and summed in bfloat16 or wider, within the bound.
A program may use at most 128 MiB of HBM per device.

```python
import jax
import jax.numpy as jnp
from jax import lax

MODEL_WIDTH = 8192
HEAD_WIDTH = 128
QUERY_HEADS = 32
KEY_VALUE_HEADS = 4
BLOCK = 128
PB_G = 32
KEEP = 8
SPAN_TOKENS = 3072
PREFIX_LENGTH = 32768
N_CTX = 8


def keep_plan(key):
    key_count, key_top, key_low, key_order = jax.random.split(key, 4)
    counts = jax.random.randint(key_count, (N_CTX,), KEEP // 4, KEEP // 2 + 1)
    busiest = jax.random.randint(key_top, (), 0, N_CTX)
    lightest = (busiest + jax.random.randint(key_low, (), 1, N_CTX)) % N_CTX
    counts = counts.at[busiest].set(KEEP).at[lightest].set(KEEP // 4)
    orders = jax.vmap(lambda sub_key: jax.random.permutation(sub_key, PB_G))(jax.random.split(key_order, N_CTX))
    chosen = orders[:, :KEEP]
    slot_index = jnp.arange(KEEP, dtype=jnp.int32)
    marked = jnp.where(slot_index[None, :] < counts[:, None], chosen, PB_G)
    ordered = jnp.sort(marked, axis=1)
    blocks = jnp.where(ordered < PB_G, ordered, 0)
    return (blocks.astype(jnp.int32), counts.astype(jnp.int32))


def draw_keep_blocks(key, part):
    return keep_plan(key)[0]


def draw_kept_counts(key, part):
    return keep_plan(key)[1]


def draw_cached_key_rows(key, part):
    key = jax.random.fold_in(key, 7)
    key_rotary_base = jax.random.fold_in(key, 0)
    rotary_base = jax.random.normal(key_rotary_base, (PREFIX_LENGTH, KEY_VALUE_HEADS * HEAD_WIDTH), jnp.float32)
    return jnp.clip(rotary_base, -256.0, 256.0).astype(jnp.bfloat16)


def with_spikes(result, stream_key, source, target, shards_of, factor):
    owner, partner = [(jnp.arange(result.shape[dim]) // (result.shape[dim] // shards_of)).reshape([-1 if axis == dim else 1 for axis in range(result.ndim)]) for dim in (source, target)]
    chosen = jax.random.permutation(stream_key, shards_of)[partner]
    strong = (owner == chosen) | (owner == (partner + shards_of // 2) % shards_of)
    return jnp.where(strong, factor * result, result)


def level_of(stream_key, dims, cuts, smallest, largest):
    def one(position, shards_of):
        steps = jax.random.uniform(jax.random.fold_in(jax.random.fold_in(stream_key, 6), position), (shards_of,), jnp.float32, smallest / len(cuts), largest / len(cuts))
        return jnp.repeat(jnp.exp(steps), dims[position] // shards_of).reshape((-1,) + (1,) * (len(dims) - position - 1))

    level = one(*cuts[0])
    for cut in cuts[1:]:
        level = level * one(*cut)
    return level


def centred(rng, extent, deviation, reach, cuts=(), held_as=jnp.bfloat16):
    drawn = jax.random.normal(rng, extent, jnp.float32) * deviation
    if len(cuts) > 0:
        drawn = level_of(rng, extent, cuts, -0.22, 0.18) * drawn
    return jnp.clip(drawn, min=-reach, max=reach).astype(held_as)


def heavy_noise(stream_key, extent, scale, most, cuts, heavy, kind=jnp.bfloat16):
    array = scale * jax.random.normal(stream_key, extent, jnp.float32)
    if cuts:
        array = array * level_of(stream_key, extent, cuts, -0.22, 0.18)
    return jnp.clip(with_spikes(array, jax.random.fold_in(stream_key, 3), *heavy), -most, most).astype(kind)


def setup_inputs(seed: int = 0) -> dict:
    key_list = jax.random.split(jax.random.key(seed), 15)
    hidden = centred(key_list[0], (SPAN_TOKENS, MODEL_WIDTH), 1.0, 6.0, ((0, 64),))
    norm_gain = jnp.clip(1.0 + 0.18 * jax.random.normal(key_list[1], (MODEL_WIDTH,), jnp.float32), 0.099609375, 1.8984375).astype(jnp.bfloat16)
    q_weight = centred(key_list[2], (MODEL_WIDTH, QUERY_HEADS * HEAD_WIDTH), (MODEL_WIDTH // 2) ** -0.5, 0.09375, ((1, 32),))
    q_bias = centred(key_list[3], (QUERY_HEADS * HEAD_WIDTH,), 0.5, 3.0, ((0, 32),))
    key_weight = centred(key_list[4], (MODEL_WIDTH, KEY_VALUE_HEADS * HEAD_WIDTH), MODEL_WIDTH ** -0.5, 0.0625, ((1, 4),))
    key_bias = centred(key_list[5], (KEY_VALUE_HEADS * HEAD_WIDTH,), 0.5, 3.0, ((0, 4),))
    value_weight = centred(key_list[6], (MODEL_WIDTH, KEY_VALUE_HEADS * HEAD_WIDTH), MODEL_WIDTH ** -0.5, 0.0625, ((1, 4),))
    value_bias = centred(key_list[7], (KEY_VALUE_HEADS * HEAD_WIDTH,), 0.5, 3.0, ((0, 4),))
    o_weight = heavy_noise(key_list[8], (QUERY_HEADS * HEAD_WIDTH, MODEL_WIDTH), (max(1, QUERY_HEADS * HEAD_WIDTH // 1024)) ** -0.5, 6.0, ((0, 32),), (0, 1, 32, 2.75))
    cached_key_rows = draw_cached_key_rows(jax.random.fold_in(key_list[14], 71), 0)
    cached_value_rows = centred(key_list[10], (PREFIX_LENGTH, KEY_VALUE_HEADS * HEAD_WIDTH), 1.0, 6.0, ((0, 8), (1, 4)))
    keep_blocks = draw_keep_blocks(jax.random.fold_in(key_list[14], 71), 0)
    kept_counts = draw_kept_counts(jax.random.fold_in(key_list[14], 71), 0)
    span_start = jax.random.randint(key_list[13], (1,), PREFIX_LENGTH, PREFIX_LENGTH + 4096).astype(jnp.int32)
    return {"hidden": hidden, "norm_gain": norm_gain, "q_weight": q_weight, "q_bias": q_bias, "key_weight": key_weight, "key_bias": key_bias, "value_weight": value_weight, "value_bias": value_bias, "o_weight": o_weight, "cached_key_rows": cached_key_rows, "cached_value_rows": cached_value_rows, "keep_blocks": keep_blocks, "kept_counts": kept_counts, "span_start": span_start}


def apply_rotary(values, token_positions):
    middle = values.shape[-1] // 2
    steps_range = jnp.arange(middle, dtype=jnp.float32)
    frequency = 1000000.0 ** (-2.0 * steps_range / values.shape[-1])
    angles = token_positions.astype(jnp.float32)[:, None] * frequency[None, :]
    cosine = jnp.cos(angles)[:, None, :]
    sine_part = jnp.sin(angles)[:, None, :]
    first_half = values[..., :middle]
    second_half = values[..., middle:]
    return jnp.concatenate([first_half * cosine - second_half * sine_part, second_half * cosine + first_half * sine_part], axis=-1)

def reference(hidden, norm_gain, q_weight, q_bias, key_weight, key_bias, value_weight, value_bias, o_weight, cached_key_rows, cached_value_rows, keep_blocks, kept_counts, span_start):
    widened = hidden.astype(jnp.float32)
    rms_factor = lax.rsqrt(lax.optimization_barrier(jnp.mean(widened * widened, axis=-1, keepdims=True)) + 1e-06)
    normed = (widened * rms_factor * norm_gain.astype(jnp.float32)).astype(jnp.bfloat16)
    token_positions = span_start[0] + jnp.arange(SPAN_TOKENS, dtype=jnp.int32)
    queries = jnp.dot(normed, q_weight, preferred_element_type=jnp.float32) + q_bias.astype(jnp.float32)
    queries = apply_rotary(queries.reshape(SPAN_TOKENS, QUERY_HEADS, HEAD_WIDTH), token_positions).astype(jnp.bfloat16)
    fresh_keys = jnp.dot(normed, key_weight, preferred_element_type=jnp.float32) + key_bias.astype(jnp.float32)
    fresh_keys = apply_rotary(fresh_keys.reshape(SPAN_TOKENS, KEY_VALUE_HEADS, HEAD_WIDTH), token_positions).astype(jnp.bfloat16)
    fresh_values = (jnp.dot(normed, value_weight, preferred_element_type=jnp.float32) + value_bias.astype(jnp.float32)).astype(jnp.bfloat16)
    fresh_values = fresh_values.reshape(SPAN_TOKENS, KEY_VALUE_HEADS, HEAD_WIDTH)
    slot_index = jnp.arange(KEEP, dtype=jnp.int32)
    block_ids = jnp.arange(N_CTX, dtype=jnp.int32)[:, None] * PB_G + keep_blocks.astype(jnp.int32)
    row_numbers = (block_ids[:, :, None] * BLOCK + jnp.arange(BLOCK, dtype=jnp.int32)[None, None, :]).reshape(-1)
    live_slots = jnp.broadcast_to((slot_index[None, :] < kept_counts[:, None])[:, :, None], (N_CTX, KEEP, BLOCK)).reshape(-1)
    retained_keys = jnp.take(cached_key_rows, row_numbers, axis=0).reshape(-1, KEY_VALUE_HEADS, HEAD_WIDTH)
    retained_values = jnp.take(cached_value_rows, row_numbers, axis=0).reshape(-1, KEY_VALUE_HEADS, HEAD_WIDTH)
    causal_mask = jnp.arange(SPAN_TOKENS)[:, None] >= jnp.arange(SPAN_TOKENS)[None, :]
    query_group_width = QUERY_HEADS // KEY_VALUE_HEADS
    score_scale = 1.0 / HEAD_WIDTH ** 0.5

    def one_head(head_index):
        kv_head = head_index // query_group_width
        query_rows = lax.dynamic_index_in_dim(queries, head_index, 1, keepdims=False)
        prefix_keys = lax.dynamic_index_in_dim(retained_keys, kv_head, 1, keepdims=False)
        prefix_values = lax.dynamic_index_in_dim(retained_values, kv_head, 1, keepdims=False)
        span_keys = lax.dynamic_index_in_dim(fresh_keys, kv_head, 1, keepdims=False)
        span_values = lax.dynamic_index_in_dim(fresh_values, kv_head, 1, keepdims=False)
        prefix_scores = jnp.dot(query_rows, prefix_keys.T, preferred_element_type=jnp.float32) * score_scale
        span_scores = jnp.dot(query_rows, span_keys.T, preferred_element_type=jnp.float32) * score_scale
        prefix_scores = jnp.where(live_slots[None, :], prefix_scores, -jnp.inf)
        span_scores = jnp.where(causal_mask, span_scores, -jnp.inf)
        row_top = jnp.maximum(prefix_scores.max(axis=-1), span_scores.max(axis=-1))[:, None]
        prefix_exp = jnp.exp(prefix_scores - row_top)
        span_exp = jnp.exp(span_scores - row_top)
        denominator = prefix_exp.sum(axis=-1) + span_exp.sum(axis=-1)
        blended = jnp.dot(prefix_exp.astype(jnp.bfloat16), prefix_values, preferred_element_type=jnp.float32)
        blended = blended + jnp.dot(span_exp.astype(jnp.bfloat16), span_values, preferred_element_type=jnp.float32)
        return (blended / denominator[:, None]).astype(jnp.bfloat16)
    heads_out = lax.map(one_head, jnp.arange(QUERY_HEADS, dtype=jnp.int32))
    attended = jnp.transpose(heads_out, (1, 0, 2)).reshape(SPAN_TOKENS, QUERY_HEADS * HEAD_WIDTH)
    return jnp.dot(attended, o_weight, preferred_element_type=jnp.float32).astype(jnp.bfloat16)
```

```python
import math

import jax
import jax.numpy as jnp
from jax import lax
from jax.experimental import pallas as pl
from jax.experimental.pallas import tpu as pltpu
from jax.sharding import PartitionSpec as P

MESH = pl.DeviceIdType.MESH
F32 = jnp.float32
BF16 = jnp.bfloat16

N_CTX = 8
WIDTH = 8192
HALF = 4096
QUART = 2048
HEAD = 128
BLOCK = 128
KEEP = 8
SHARDS = 8
SHARD = 48
CHUNKS = 3
PIECE = 16
CHUNK = SHARDS * PIECE
GROUP = SHARDS * SHARD
KEPT = KEEP * BLOCK
NEG = -1e30
LOG2E = math.log2(math.e)


def nt_dot(a, b):
    return lax.dot_general(a, b, (((1,), (1,)), ((), ())), preferred_element_type=F32)


def nn_dot(a, b):
    return lax.dot_general(a, b, (((1,), (0,)), ((), ())), preferred_element_type=F32)


def keep_kernel(blocks_ref, counts_ref, k_ref, v_ref, kept_k_ref, kept_v_ref, mask_ref, sems):
    copies = []
    for j in range(KEEP):
        source = pl.ds(pl.multiple_of(blocks_ref[0, j] * BLOCK, BLOCK), BLOCK)
        for i, (whole, kept) in enumerate(((k_ref, kept_k_ref), (v_ref, kept_v_ref))):
            copy = pltpu.make_async_copy(whole.at[source, :], kept.at[pl.ds(j * BLOCK, BLOCK), :], sems.at[i, j])
            copy.start()
            copies.append(copy)
    z = lax.axis_index("ctx")
    for s in range(3):
        live = counts_ref[lax.rem(z + s + 7, 8)]
        slot = lax.broadcasted_iota(jnp.int32, (1, KEPT), 1) // BLOCK
        mask_ref[s] = jnp.where(slot < live, 0.0, NEG).astype(F32)
    for copy in copies:
        copy.wait()


def kernel(
    hidden_ref, gain_ref, qw_ref, qb_ref, kw_ref, kb_ref, vw_ref, vb_ref, ow_ref, kept_k_ref, kept_v_ref,
    mask, cos_ref, sin_ref,
    out_ref,
    normed, gathered, q_mat, kv_mat, o_mat,
    pre_k, pre_v, span_k, span_v,
    halves, halves_in, queries, part_o, part_s, part_o_in, part_s_in,
    own_o, own_m, attended, one_out, one_in, mid, two_out, two_in,
    local_sems, a_send, a_recv, w_send, w_recv, pre_send, pre_recv, row_send, row_recv, span_send, span_recv,
    h_send, h_recv, q_send, q_recv, p_send, p_recv, t_send, t_recv, one_send, one_recv, two_send, two_recv,
):
    z = lax.axis_index("ctx")
    head = lax.axis_index("head")
    row = lax.axis_index("row")
    core = lax.rem(head, 2)
    x_lo = row // 4
    y = lax.rem(row, 4)
    x = 2 * (head // 2) + x_lo
    other = 1 - core

    def device(dz, dx, dy, dc=None):
        xx = lax.rem(x + dx + 4, 4)
        yy = lax.rem(y + dy + 4, 4)
        cc = core if dc is None else dc
        return (lax.rem(z + dz + 8, 8), 2 * (xx // 2) + cc, 4 * lax.rem(xx, 2) + yy)

    def row_peer(step):
        return (z, head, lax.rem(row + step, SHARDS))

    partner = (z, 2 * (head // 2) + other, row)

    def remote(src, dst, send, recv, to):
        return pltpu.make_async_remote_copy(
            src_ref=src, dst_ref=dst, send_sem=send, recv_sem=recv, device_id=to, device_id_type=MESH
        )

    sent = []

    def send(src, dst, send_sem, recv_sem, to):
        copy = remote(src, dst, send_sem, recv_sem, to)
        copy.start()
        sent.append(copy)

    def arrive(dst, recv_sem):
        remote(dst, dst, recv_sem, recv_sem, partner).wait_recv()

    def load(src, dst, i):
        copy = pltpu.make_async_copy(src, dst, local_sems.at[i])
        copy.start()
        return copy

    load_k = load(kept_k_ref, pre_k.at[1], 0)
    load_v = load(kept_v_ref, pre_v.at[1, :, 0:HEAD], 1)
    load_kw = load(kw_ref, kv_mat.at[:, 0:HEAD], 2)
    load_vw = load(vw_ref, kv_mat.at[:, HEAD : 2 * HEAD], 3)
    own_cols = pl.ds(pl.multiple_of(core * HEAD, HEAD), HEAD)
    load_qw = load(qw_ref.at[pl.ds(pl.multiple_of(core * HALF, HALF), HALF), :], q_mat.at[:, own_cols], 4)

    def column(cc, first, second):
        xx = first * (1 - cc) + second * cc
        yy = second * (1 - cc) + first * cc
        return pl.multiple_of((2 * (xx // 2) + cc) * 2048 + (4 * lax.rem(xx, 2) + yy) * 256, 256)

    for b1 in range(4):
        for b2 in range(4):
            pltpu.make_async_copy(
                ow_ref.at[:, pl.ds(column(core, b1, b2), 256)],
                o_mat.at[b1, own_cols, pl.ds(b2 * 256, 256)],
                local_sems.at[5],
            ).start()

    barrier = pltpu.get_barrier_semaphore()
    partners = [partner]
    partners += [device(0, 1, 0), device(0, -1, 0)]
    partners += [row_peer(s) for s in range(1, SHARDS)]
    partners += [device(dz, 0, 0) for dz in (1, -1, 3, -3)]
    for to in partners:
        pl.semaphore_signal(barrier, inc=1, device_id=to, device_id_type=MESH)
    pl.semaphore_wait(barrier, len(partners))

    total = jnp.zeros((SHARD, 1), F32)
    for i in range(8):
        part = hidden_ref[:, i * 1024 : (i + 1) * 1024].astype(F32)
        total = total + jnp.sum(part * part, axis=1, keepdims=True)
    factor = lax.rsqrt(total / WIDTH + 1e-6)
    for i in range(8):
        cols = slice(i * 1024, (i + 1) * 1024)
        part = hidden_ref[:, cols].astype(F32) * factor * gain_ref[:, cols].astype(F32)
        normed[:, cols] = part.astype(BF16)

    def rows_of(shard):
        return pl.ds(pl.multiple_of(shard * PIECE, PIECE), PIECE)

    for k in range(CHUNKS):
        for f in range(2):
            cols = pl.ds(pl.multiple_of(core * HALF + f * QUART, QUART), QUART)
            gathered[k, f, rows_of(row), :] = normed[k * PIECE : (k + 1) * PIECE, cols]

    y_up, y_down = device(0, 0, 1), device(0, 0, -1)
    x_up, x_down = device(0, 1, 0), device(0, -1, 0)
    a_count = [0, 0, 0]

    def forward(k, f, shard, to):
        piece = gathered.at[k, f, rows_of(shard), :]
        send(piece, piece, a_send.at[k, a_count[k]], a_recv.at[k, f, shard], to)
        a_count[k] += 1

    def shard_at(dy, flip=False):
        xl = 1 - x_lo if flip else x_lo
        return 4 * xl + lax.rem(y + dy + 4, 4)

    def a_arrive(k, f, shard):
        arrive(gathered.at[k, f, rows_of(shard), :], a_recv.at[k, f, shard])

    def a_start(k):
        forward(k, 0, row, x_up)
        forward(k, 0, row, y_up)
        forward(k, 1, row, x_down)
        forward(k, 1, row, y_down)
        forward(k, 1, row, y_up)
        forward(k, 0, row, y_down)

    def a_mid(k):
        below, above = shard_at(-1), shard_at(1)
        a_arrive(k, 0, below)
        forward(k, 0, below, y_up)
        forward(k, 0, below, x_up)
        a_arrive(k, 1, above)
        forward(k, 1, above, y_down)
        forward(k, 1, above, x_down)
        a_arrive(k, 1, below)
        forward(k, 1, below, x_down)
        a_arrive(k, 0, above)
        forward(k, 0, above, x_up)

    def a_last(k):
        far = shard_at(2)
        a_arrive(k, 0, far)
        forward(k, 0, far, x_up)
        a_arrive(k, 1, far)
        forward(k, 1, far, x_down)

    for k in range(CHUNKS):
        a_start(k)

    send(
        qw_ref.at[pl.ds(pl.multiple_of(other * HALF, HALF), HALF), :],
        q_mat.at[:, own_cols], w_send.at[0], w_recv.at[0], partner,
    )
    for b1 in range(4):
        for b2 in range(4):
            remote(
                ow_ref.at[:, pl.ds(column(other, b1, b2), 256)],
                o_mat.at[b1, own_cols, pl.ds(b2 * 256, 256)],
                w_send.at[1], w_recv.at[1], partner,
            ).start()

    load_k.wait()
    load_v.wait()
    z_up, z_down = device(1, 0, 0), device(-1, 0, 0)
    left = pl.ds(0, HEAD)
    for i, (slot, to) in enumerate(((0, z_up), (2, z_down))):
        send(pre_k.at[1], pre_k.at[slot], pre_send.at[0, i], pre_recv.at[0, slot], to)
        send(pre_v.at[1, :, left], pre_v.at[slot, :, left], pre_send.at[1, i], pre_recv.at[1, slot], to)

    for s in range(3):
        pre_v[s, :, HEAD : 2 * HEAD] = jnp.ones((KEPT, HEAD), BF16)
        span_v[s, :, HEAD : 2 * HEAD] = jnp.ones((GROUP, HEAD), BF16)

    def rotated(values, cosine, sine):
        return values * cosine + pltpu.roll(values, HEAD // 2, 1) * sine

    load_kw.wait()
    load_vw.wait()

    def kv_step(i, total):
        at = pl.ds(pl.multiple_of(i * 1024, 1024), 1024)
        return total + nn_dot(normed[:, at], kv_mat[at, :])

    pair = lax.fori_loop(0, 8, kv_step, jnp.zeros((SHARD, 2 * HEAD), F32))
    key_part = pair[:, 0:HEAD] + kb_ref[...].astype(F32)
    value_part = pair[:, HEAD : 2 * HEAD] + vb_ref[...].astype(F32)
    own_cos = jnp.concatenate([cos_ref[k, rows_of(row), :] for k in range(CHUNKS)], axis=0)
    own_sin = jnp.concatenate([sin_ref[k, rows_of(row), :] for k in range(CHUNKS)], axis=0)

    def span_rows(shard):
        return pl.ds(pl.multiple_of(shard * SHARD, SHARD), SHARD)

    span_k[1, span_rows(row), :] = rotated(key_part, own_cos, own_sin).astype(BF16)
    span_v[1, span_rows(row), 0:HEAD] = value_part.astype(BF16)
    for s in range(1, SHARDS):
        here = span_k.at[1, span_rows(row), :]
        send(here, here, row_send.at[0, s], row_recv.at[0, row], row_peer(s))
        here = span_v.at[1, span_rows(row), left]
        send(here, here, row_send.at[1, s], row_recv.at[1, row], row_peer(s))

    def span_forward():
        for s in range(1, SHARDS):
            peer = lax.rem(row + s, SHARDS)
            arrive(span_k.at[1, span_rows(peer), :], row_recv.at[0, peer])
            arrive(span_v.at[1, span_rows(peer), left], row_recv.at[1, peer])
        for i, (slot, to) in enumerate(((0, z_up), (2, z_down))):
            send(span_k.at[1], span_k.at[slot], span_send.at[0, i], span_recv.at[0, slot], to)
            send(span_v.at[1, :, left], span_v.at[slot, :, left], span_send.at[1, i], span_recv.at[1, slot], to)

    def neighbours_arrive():
        for slot in (0, 2):
            arrive(pre_k.at[slot], pre_recv.at[0, slot])
            arrive(pre_v.at[slot, :, left], pre_recv.at[1, slot])
            arrive(span_k.at[slot], span_recv.at[0, slot])
            arrive(span_v.at[slot, :, left], span_recv.at[1, slot])

    def project(k):
        for shard_dy in range(4):
            for f in range(2):
                a_arrive(k, f, shard_at(shard_dy, True))
        both = nn_dot(gathered[k, 0], q_mat[0:QUART, :]) + nn_dot(gathered[k, 1], q_mat[QUART:HALF, :])
        halves[k, 0] = both[:, 0:HEAD]
        halves[k, 1] = both[:, HEAD : 2 * HEAD]
        send(halves.at[k, other], halves_in.at[k], h_send.at[k], h_recv.at[k], partner)

    def finish_queries(k):
        arrive(halves_in.at[k], h_recv.at[k])
        values = halves[k, core] + halves_in[k] + qb_ref[...].astype(F32)
        values = rotated(values, cos_ref[k], sin_ref[k]) * (LOG2E / math.sqrt(HEAD))
        queries[0, k] = values.astype(BF16)
        send(queries.at[0, k], queries.at[1, k], q_send.at[k, 0], q_recv.at[k, 0], device(3, 0, 0))
        send(queries.at[0, k], queries.at[2, k], q_send.at[k, 1], q_recv.at[k, 1], device(-3, 0, 0))

    token = lax.broadcasted_iota(jnp.int32, (CHUNK, 1), 0)
    token = (token // PIECE) * SHARD + lax.rem(token, PIECE)
    key_token = lax.broadcasted_iota(jnp.int32, (1, GROUP), 1)

    def attend(k, source, first, last):
        query = queries[source, k]
        query_group = lax.rem(z + (0, 5, 3)[source], 8)
        query_token = query_group * GROUP + k * PIECE + token

        def over(slot, total, top):
            prefix = nt_dot(query, pre_k[slot]) + mask[slot]
            span = nt_dot(query, span_k[slot])
            key_group = lax.rem(z + slot + 7, 8)
            span = jnp.where(key_group * GROUP + key_token <= query_token, span, NEG)
            new_top = jnp.maximum(
                jnp.max(prefix, axis=1, keepdims=True), jnp.max(span, axis=1, keepdims=True)
            )
            if top is not None:
                new_top = jnp.maximum(new_top, top)
            blended = nn_dot(jnp.exp2(prefix - new_top).astype(BF16), pre_v[slot])
            blended = blended + nn_dot(jnp.exp2(span - new_top).astype(BF16), span_v[slot])
            if top is not None:
                blended = blended + total * jnp.exp2(top - new_top)
            return blended, new_top

        state = over(first, None, None)
        return lax.fori_loop(first + 1, last, lambda s, c: over(s, *c), state)

    def attend_own(k):
        total, top = attend(k, 0, 0, 3)
        own_o[k] = total
        own_m[k] = jnp.broadcast_to(top, (CHUNK, HEAD))

    def attend_other(k):
        for i, (source, first) in enumerate(((1, 0), (2, 1))):
            arrive(queries.at[source, k], q_recv.at[k, i])
            total, top = attend(k, source, first, 3)
            part_o[k, i] = total[:, 0:HEAD].astype(BF16)
            part_s[k, i, 0:4, :] = jnp.transpose(jnp.broadcast_to(top, (CHUNK, HEAD)))[0:4, :]
            part_s[k, i, 4:8, :] = jnp.transpose(total[:, HEAD : 2 * HEAD])[0:4, :]
            back = device(-3 if source == 1 else 3, 0, 0)
            send(part_o.at[k, i], part_o_in.at[k, i], p_send.at[k, i, 0], p_recv.at[k, i, 0], back)
            send(part_s.at[k, i], part_s_in.at[k, i], p_send.at[k, i, 1], p_recv.at[k, i, 1], back)

    def combine(k):
        total, low, top = own_o[k][:, 0:HEAD], own_o[k][:, HEAD : 2 * HEAD], own_m[k]
        for i in range(2):
            arrive(part_o_in.at[k, i], p_recv.at[k, i, 0])
            arrive(part_s_in.at[k, i], p_recv.at[k, i, 1])
            their_top = jnp.transpose(jnp.broadcast_to(part_s_in[k, i, 0:1, :], (CHUNK, HEAD)))
            their_low = jnp.transpose(jnp.broadcast_to(part_s_in[k, i, 4:5, :], (CHUNK, HEAD)))
            new_top = jnp.maximum(top, their_top)
            mine, theirs = jnp.exp2(top - new_top), jnp.exp2(their_top - new_top)
            total = total * mine + part_o_in[k, i].astype(F32) * theirs
            low = low * mine + their_low * theirs
            top = new_top
        attended[k, :, own_cols] = (total / low).astype(BF16)
        here = attended.at[k, :, own_cols]
        send(here, here, t_send.at[k], t_recv.at[k], partner)

    first = x * other + y * core
    second = y * other + x * core

    def ring(stage, direction):
        step = 1 - 2 * direction
        along_x = other if stage == 0 else core
        return device(0, step * along_x, step * (1 - along_x))

    def chunk_rows(d):
        return slice(d * 64, (d + 1) * 64)

    def target(index, d, s):
        return lax.rem(index - 1 - s + 4, 4) if d == 0 else lax.rem(index + 1 + s, 4)

    def product(k, d, block):
        return nn_dot(attended[k, chunk_rows(d), :], o_mat[block])

    def attended_arrive(k):
        arrive(attended.at[k, :, pl.ds(pl.multiple_of(other * HEAD, HEAD), HEAD)], t_recv.at[k])

    def stage_one(k, s):
        for d in range(2):
            value = product(k, d, first if s == 3 else target(first, d, s))
            if s > 0:
                arrive(one_in.at[k, d, s - 1], one_recv.at[k, d, s - 1])
                value = value + one_in[k, d, s - 1].astype(F32)
            if s < 3:
                one_out[k, d, s] = value.astype(BF16)
                send(one_out.at[k, d, s], one_in.at[k, d, s], one_send.at[k, d, s], one_recv.at[k, d, s], ring(0, d))
            else:
                for b in range(4):
                    mid[k, d, b] = value[:, b * 256 : (b + 1) * 256]

    def stage_two(k, s):
        for d in range(2):
            value = mid[k, d, second if s == 3 else target(second, d, s)]
            if s > 0:
                arrive(two_in.at[k, d, s - 1], two_recv.at[k, d, s - 1])
                value = value + two_in[k, d, s - 1].astype(F32)
            if s < 3:
                two_out[k, d, s] = value.astype(BF16)
                send(two_out.at[k, d, s], two_in.at[k, d, s], two_send.at[k, d, s], two_recv.at[k, d, s], ring(1, d))
            else:
                result = value.astype(BF16)
                for i in range(4):
                    at = (4 * d + i) * SHARD + k * PIECE
                    out_ref[at : at + PIECE, :] = result[i * PIECE : (i + 1) * PIECE, :]

    a_mid(0)
    span_forward()
    a_mid(1)
    a_last(0)
    load_qw.wait()
    arrive(q_mat.at[:, pl.ds(pl.multiple_of(other * HEAD, HEAD), HEAD)], w_recv.at[0])
    project(0)
    a_mid(2)
    a_last(1)
    finish_queries(0)
    project(1)
    a_last(2)
    finish_queries(1)
    neighbours_arrive()
    attend_own(0)
    attend_other(0)
    project(2)
    attend_own(1)
    finish_queries(2)
    pltpu.make_async_copy(o_mat.at[:, own_cols, :], o_mat.at[:, own_cols, :], local_sems.at[5]).wait()
    arrive(o_mat.at[:, pl.ds(pl.multiple_of(other * HEAD, HEAD), HEAD), :], w_recv.at[1])
    combine(0)
    attend_other(1)
    attended_arrive(0)
    stage_one(0, 0)
    attend_own(2)
    stage_one(0, 1)
    combine(1)
    attend_other(2)
    stage_one(0, 2)
    attended_arrive(1)
    stage_one(1, 0)
    stage_one(0, 3)
    stage_two(0, 0)
    combine(2)
    stage_one(1, 1)
    stage_two(0, 1)
    attended_arrive(2)
    stage_one(2, 0)
    stage_one(1, 2)
    stage_two(0, 2)
    stage_one(2, 1)
    stage_one(1, 3)
    stage_two(1, 0)
    stage_two(0, 3)
    stage_one(2, 2)
    stage_two(1, 1)
    stage_one(2, 3)
    stage_two(2, 0)
    stage_two(1, 2)
    stage_two(2, 1)
    stage_two(1, 3)
    stage_two(2, 2)
    stage_two(2, 3)

    for copy in sent:
        copy.wait_send()
    theirs = o_mat.at[:, pl.ds(pl.multiple_of(other * HEAD, HEAD), HEAD), :]
    remote(theirs, theirs, w_send.at[1], w_recv.at[1], partner).wait_send()


def local(
    hidden, norm_gain, q_weight, q_bias, key_weight, key_bias, value_weight, value_bias, o_weight,
    cached_key_rows, cached_value_rows, keep_blocks, kept_counts, span_start,
):
    group = lax.axis_index("ctx")
    token = jnp.arange(CHUNKS * CHUNK, dtype=jnp.int32)
    token = (token % CHUNK // PIECE) * SHARD + token // CHUNK * PIECE + token % PIECE
    positions = span_start[0] + group * GROUP + token
    steps = jnp.arange(HEAD // 2, dtype=F32)
    frequency = 1000000.0 ** (-2.0 * steps / HEAD)
    angles = positions.astype(F32)[:, None] * frequency[None, :]
    cosine, sine = jnp.cos(angles), jnp.sin(angles)
    cosine = jnp.concatenate([cosine, cosine], axis=1).reshape(CHUNKS, CHUNK, HEAD)
    sine = jnp.concatenate([-sine, sine], axis=1).reshape(CHUNKS, CHUNK, HEAD)

    vmem = pl.BlockSpec(memory_space=pltpu.VMEM)
    smem = pl.BlockSpec(memory_space=pltpu.SMEM)
    hbm = pl.BlockSpec(memory_space=pl.ANY)
    dma = pltpu.SemaphoreType.DMA
    kept = jax.ShapeDtypeStruct((KEPT, HEAD), BF16)
    kept_k, kept_v, mask = pl.pallas_call(
        keep_kernel,
        out_shape=(kept, kept, jax.ShapeDtypeStruct((3, 1, KEPT), F32)),
        in_specs=[smem, smem, hbm, hbm],
        out_specs=(vmem, vmem, vmem),
        scratch_shapes=[dma((2, KEEP))],
        name="kept_blocks",
    )(keep_blocks, kept_counts, cached_key_rows, cached_value_rows)
    scratch = [
        pltpu.VMEM((SHARD, WIDTH), BF16),
        pltpu.VMEM((CHUNKS, 2, CHUNK, QUART), BF16),
        pltpu.VMEM((HALF, 2 * HEAD), BF16),
        pltpu.VMEM((WIDTH, 2 * HEAD), BF16),
        pltpu.VMEM((4, 2 * HEAD, 1024), BF16),
        pltpu.VMEM((3, KEPT, HEAD), BF16),
        pltpu.VMEM((3, KEPT, 2 * HEAD), BF16),
        pltpu.VMEM((3, GROUP, HEAD), BF16),
        pltpu.VMEM((3, GROUP, 2 * HEAD), BF16),
        pltpu.VMEM((CHUNKS, 2, CHUNK, HEAD), F32),
        pltpu.VMEM((CHUNKS, CHUNK, HEAD), F32),
        pltpu.VMEM((3, CHUNKS, CHUNK, HEAD), BF16),
        pltpu.VMEM((CHUNKS, 2, CHUNK, HEAD), BF16),
        pltpu.VMEM((CHUNKS, 2, 8, CHUNK), F32),
        pltpu.VMEM((CHUNKS, 2, CHUNK, HEAD), BF16),
        pltpu.VMEM((CHUNKS, 2, 8, CHUNK), F32),
        pltpu.VMEM((CHUNKS, CHUNK, 2 * HEAD), F32),
        pltpu.VMEM((CHUNKS, CHUNK, HEAD), F32),
        pltpu.VMEM((CHUNKS, CHUNK, 2 * HEAD), BF16),
        pltpu.VMEM((CHUNKS, 2, 3, 64, 1024), BF16),
        pltpu.VMEM((CHUNKS, 2, 3, 64, 1024), BF16),
        pltpu.VMEM((CHUNKS, 2, 4, 64, 256), F32),
        pltpu.VMEM((CHUNKS, 2, 3, 64, 256), BF16),
        pltpu.VMEM((CHUNKS, 2, 3, 64, 256), BF16),
        dma((6,)),
        dma((CHUNKS, 14)), dma((CHUNKS, 2, SHARDS)),
        dma((2,)), dma((2,)),
        dma((2, 2)), dma((2, 3)),
        dma((2, SHARDS)), dma((2, SHARDS)),
        dma((2, 2)), dma((2, 3)),
        dma((CHUNKS,)), dma((CHUNKS,)),
        dma((CHUNKS, 2)), dma((CHUNKS, 2)),
        dma((CHUNKS, 2, 2)), dma((CHUNKS, 2, 2)),
        dma((CHUNKS,)), dma((CHUNKS,)),
        dma((CHUNKS, 2, 3)), dma((CHUNKS, 2, 3)),
        dma((CHUNKS, 2, 3)), dma((CHUNKS, 2, 3)),
    ]
    return pl.pallas_call(
        kernel,
        out_shape=jax.ShapeDtypeStruct((GROUP, 256), BF16),
        in_specs=[vmem, vmem, hbm, vmem, hbm, vmem, hbm, vmem, hbm, hbm, hbm, vmem, vmem, vmem],
        out_specs=vmem,
        scratch_shapes=scratch,
        compiler_params=pltpu.CompilerParams(
            collective_id=0, has_side_effects=True, vmem_limit_bytes=56 * 1024 * 1024
        ),
        name="attention_sublayer",
    )(
        hidden, norm_gain.reshape(1, -1), q_weight, q_bias.reshape(1, -1), key_weight, key_bias.reshape(1, -1),
        value_weight, value_bias.reshape(1, -1), o_weight, kept_k, kept_v, mask, cosine, sine,
    )


def solution(mesh):
    in_specs = (
        P(("ctx", "row"), None),
        P(),
        P(None, ("head", "row")),
        P(("head", "row")),
        P(None, "head"),
        P("head"),
        P(None, "head"),
        P("head"),
        P(("head", "row"), None),
        P("ctx", "head"),
        P("ctx", "head"),
        P("ctx", None),
        P(),
        P(),
    )
    out_specs = P("ctx", ("head", "row"))
    return jax.shard_map(local, mesh=mesh, in_specs=in_specs, out_specs=out_specs, check_vma=False)
```

```python
import math

import jax
import jax.numpy as jnp
from jax import lax
from jax.experimental import pallas as pl
from jax.experimental.pallas import tpu as pltpu
from jax.sharding import PartitionSpec as P

MESH = pl.DeviceIdType.MESH
F32 = jnp.float32
BF16 = jnp.bfloat16

N_CTX = 8
WIDTH = 8192
HALF = 4096
QUART = 2048
HEAD = 128
BLOCK = 128
KEEP = 8
SHARDS = 8
SHARD = 48
CHUNKS = 3
PIECE = 16
CHUNK = SHARDS * PIECE
GROUP = SHARDS * SHARD
KEPT = KEEP * BLOCK
NEG = -1e30
LOG2E = math.log2(math.e)


def nt_dot(a, b):
    return lax.dot_general(a, b, (((1,), (1,)), ((), ())), preferred_element_type=F32)


def nn_dot(a, b):
    return lax.dot_general(a, b, (((1,), (0,)), ((), ())), preferred_element_type=F32)


def keep_kernel(blocks_ref, counts_ref, k_ref, v_ref, kept_k_ref, kept_v_ref, mask_ref, sems):
    copies = []
    for j in range(KEEP):
        source = pl.ds(pl.multiple_of(blocks_ref[0, j] * BLOCK, BLOCK), BLOCK)
        for i, (whole, kept) in enumerate(((k_ref, kept_k_ref), (v_ref, kept_v_ref))):
            copy = pltpu.make_async_copy(whole.at[source, :], kept.at[pl.ds(j * BLOCK, BLOCK), :], sems.at[i, j])
            copy.start()
            copies.append(copy)
    z = lax.axis_index("ctx")
    for s in range(3):
        live = counts_ref[lax.rem(z + s + 7, 8)]
        slot = lax.broadcasted_iota(jnp.int32, (1, KEPT), 1) // BLOCK
        mask_ref[s] = jnp.where(slot < live, 0.0, NEG).astype(F32)
    for copy in copies:
        copy.wait()


def kernel(
    hidden_ref, gain_ref, qw_ref, qb_ref, kw_ref, kb_ref, vw_ref, vb_ref, ow_ref, kept_k_ref, kept_v_ref,
    mask, cos_ref, sin_ref,
    out_ref,
    normed, gathered, q_mat, kv_mat, o_mat,
    pre_k, pre_v, span_k, span_v,
    halves, halves_in, queries, part_o, part_s, part_o_in, part_s_in,
    own_o, own_m, attended, one_out, one_in, mid, two_out, two_in,
    local_sems, a_send, a_recv, w_send, w_recv, pre_send, pre_recv, row_send, row_recv, span_send, span_recv,
    h_send, h_recv, q_send, q_recv, p_send, p_recv, t_send, t_recv, one_send, one_recv, two_send, two_recv,
):
    z = lax.axis_index("ctx")
    head = lax.axis_index("head")
    row = lax.axis_index("row")
    core = lax.rem(head, 2)
    x_lo = row // 4
    y = lax.rem(row, 4)
    x = 2 * (head // 2) + x_lo
    other = 1 - core

    def device(dz, dx, dy, dc=None):
        xx = lax.rem(x + dx + 4, 4)
        yy = lax.rem(y + dy + 4, 4)
        cc = core if dc is None else dc
        return (lax.rem(z + dz + 8, 8), 2 * (xx // 2) + cc, 4 * lax.rem(xx, 2) + yy)

    def row_peer(step):
        return (z, head, lax.rem(row + step, SHARDS))

    partner = (z, 2 * (head // 2) + other, row)

    def remote(src, dst, send, recv, to):
        return pltpu.make_async_remote_copy(
            src_ref=src, dst_ref=dst, send_sem=send, recv_sem=recv, device_id=to, device_id_type=MESH
        )

    sent = []

    def send(src, dst, send_sem, recv_sem, to):
        copy = remote(src, dst, send_sem, recv_sem, to)
        copy.start()
        sent.append(copy)

    def arrive(dst, recv_sem):
        remote(dst, dst, recv_sem, recv_sem, partner).wait_recv()

    def load(src, dst, i):
        copy = pltpu.make_async_copy(src, dst, local_sems.at[i])
        copy.start()
        return copy

    load_k = load(kept_k_ref, pre_k.at[1], 0)
    load_v = load(kept_v_ref, pre_v.at[1, :, 0:HEAD], 1)
    load_kw = load(kw_ref, kv_mat.at[:, 0:HEAD], 2)
    load_vw = load(vw_ref, kv_mat.at[:, HEAD : 2 * HEAD], 3)
    own_cols = pl.ds(pl.multiple_of(core * HEAD, HEAD), HEAD)
    load_qw = load(qw_ref.at[pl.ds(pl.multiple_of(core * HALF, HALF), HALF), :], q_mat.at[:, own_cols], 4)

    def column(cc, first, second):
        xx = first * (1 - cc) + second * cc
        yy = second * (1 - cc) + first * cc
        return pl.multiple_of((2 * (xx // 2) + cc) * 2048 + (4 * lax.rem(xx, 2) + yy) * 256, 256)

    for b1 in range(4):
        for b2 in range(4):
            pltpu.make_async_copy(
                ow_ref.at[:, pl.ds(column(core, b1, b2), 256)],
                o_mat.at[b1, own_cols, pl.ds(b2 * 256, 256)],
                local_sems.at[5],
            ).start()

    barrier = pltpu.get_barrier_semaphore()
    partners = [partner]
    partners += [device(0, 1, 0), device(0, -1, 0), device(0, 2, 0)]
    partners += [row_peer(s) for s in range(1, SHARDS)]
    partners += [device(dz, 0, 0) for dz in (1, -1, 3, -3)]
    for to in partners:
        pl.semaphore_signal(barrier, inc=1, device_id=to, device_id_type=MESH)
    pl.semaphore_wait(barrier, len(partners))

    def rows_of(shard):
        return pl.ds(pl.multiple_of(shard * PIECE, PIECE), PIECE)

    def normalise(k):
        rows = slice(k * PIECE, (k + 1) * PIECE)
        total = jnp.zeros((PIECE, 1), F32)
        for i in range(8):
            part = hidden_ref[rows, i * 1024 : (i + 1) * 1024].astype(F32)
            total = total + jnp.sum(part * part, axis=1, keepdims=True)
        factor = lax.rsqrt(total / WIDTH + 1e-6)
        for i in range(8):
            cols = slice(i * 1024, (i + 1) * 1024)
            part = hidden_ref[rows, cols].astype(F32) * factor * gain_ref[:, cols].astype(F32)
            normed[rows, cols] = part.astype(BF16)
        for f in range(2):
            cols = pl.ds(pl.multiple_of(core * HALF + f * QUART, QUART), QUART)
            gathered[k, f, rows_of(row), :] = normed[rows, cols]

    y_up, y_down = device(0, 0, 1), device(0, 0, -1)
    x_up, x_down = device(0, 1, 0), device(0, -1, 0)
    a_count = [0, 0, 0]

    def forward(k, f, shard, to):
        piece = gathered.at[k, f, rows_of(shard), :]
        send(piece, piece, a_send.at[k, a_count[k]], a_recv.at[k, f, shard], to)
        a_count[k] += 1

    def shard_at(dy, flip=False):
        xl = 1 - x_lo if flip else x_lo
        return 4 * xl + lax.rem(y + dy + 4, 4)

    def a_arrive(k, f, shard):
        arrive(gathered.at[k, f, rows_of(shard), :], a_recv.at[k, f, shard])

    def a_start(k):
        forward(k, 0, row, x_up)
        forward(k, 0, row, y_up)
        forward(k, 1, row, x_down)
        forward(k, 1, row, y_down)
        forward(k, 1, row, y_up)
        forward(k, 0, row, y_down)

    def a_mid(k):
        below, above = shard_at(-1), shard_at(1)
        a_arrive(k, 0, below)
        forward(k, 0, below, y_up)
        forward(k, 0, below, x_up)
        a_arrive(k, 1, above)
        forward(k, 1, above, y_down)
        forward(k, 1, above, x_down)
        a_arrive(k, 1, below)
        forward(k, 1, below, x_down)
        a_arrive(k, 0, above)
        forward(k, 0, above, x_up)

    def a_last(k):
        far = shard_at(2)
        a_arrive(k, 0, far)
        forward(k, 0, far, x_up)
        a_arrive(k, 1, far)
        forward(k, 1, far, x_down)

    normalise(0)
    a_start(0)
    normalise(1)
    a_start(1)
    normalise(2)

    send(
        qw_ref.at[pl.ds(pl.multiple_of(other * HALF, HALF), HALF), :],
        q_mat.at[:, own_cols], w_send.at[0], w_recv.at[0], partner,
    )
    for b1 in range(4):
        for b2 in range(4):
            remote(
                ow_ref.at[:, pl.ds(column(other, b1, b2), 256)],
                o_mat.at[b1, own_cols, pl.ds(b2 * 256, 256)],
                w_send.at[1], w_recv.at[1], partner,
            ).start()

    load_k.wait()
    load_v.wait()
    z_up, z_down = device(1, 0, 0), device(-1, 0, 0)
    left = pl.ds(0, HEAD)
    for i, (slot, to) in enumerate(((0, z_up), (2, z_down))):
        send(pre_k.at[1], pre_k.at[slot], pre_send.at[0, i], pre_recv.at[0, slot], to)
        send(pre_v.at[1, :, left], pre_v.at[slot, :, left], pre_send.at[1, i], pre_recv.at[1, slot], to)

    for s in range(3):
        pre_v[s, :, HEAD : 2 * HEAD] = jnp.ones((KEPT, HEAD), BF16)
        span_v[s, :, HEAD : 2 * HEAD] = jnp.ones((GROUP, HEAD), BF16)

    def rotated(values, cosine, sine):
        return values * cosine + pltpu.roll(values, HEAD // 2, 1) * sine

    load_kw.wait()
    load_vw.wait()

    def kv_step(i, total):
        at = pl.ds(pl.multiple_of(i * 1024, 1024), 1024)
        return total + nn_dot(normed[:, at], kv_mat[at, :])

    def span_rows(shard):
        return pl.ds(pl.multiple_of(shard * SHARD, SHARD), SHARD)

    pair = lax.fori_loop(0, 4, kv_step, jnp.zeros((SHARD, 2 * HEAD), F32))
    a_mid(0)
    a_start(2)
    pair = lax.fori_loop(4, 8, kv_step, pair)
    key_part = pair[:, 0:HEAD] + kb_ref[...].astype(F32)
    value_part = pair[:, HEAD : 2 * HEAD] + vb_ref[...].astype(F32)
    own_cos = jnp.concatenate([cos_ref[k, rows_of(row), :] for k in range(CHUNKS)], axis=0)
    own_sin = jnp.concatenate([sin_ref[k, rows_of(row), :] for k in range(CHUNKS)], axis=0)

    span_k[1, span_rows(row), :] = rotated(key_part, own_cos, own_sin).astype(BF16)
    span_v[1, span_rows(row), 0:HEAD] = value_part.astype(BF16)
    for s in range(1, SHARDS):
        here = span_k.at[1, span_rows(row), :]
        send(here, here, row_send.at[0, s], row_recv.at[0, row], row_peer(s))
        here = span_v.at[1, span_rows(row), left]
        send(here, here, row_send.at[1, s], row_recv.at[1, row], row_peer(s))

    def span_forward():
        for s in range(1, SHARDS):
            peer = lax.rem(row + s, SHARDS)
            arrive(span_k.at[1, span_rows(peer), :], row_recv.at[0, peer])
            arrive(span_v.at[1, span_rows(peer), left], row_recv.at[1, peer])
        for i, (slot, to) in enumerate(((0, z_up), (2, z_down))):
            send(span_k.at[1], span_k.at[slot], span_send.at[0, i], span_recv.at[0, slot], to)
            send(span_v.at[1, :, left], span_v.at[slot, :, left], span_send.at[1, i], span_recv.at[1, slot], to)

    def neighbours_arrive():
        for slot in (0, 2):
            arrive(pre_k.at[slot], pre_recv.at[0, slot])
            arrive(pre_v.at[slot, :, left], pre_recv.at[1, slot])
            arrive(span_k.at[slot], span_recv.at[0, slot])
            arrive(span_v.at[slot, :, left], span_recv.at[1, slot])

    def project(k):
        for shard_dy in range(4):
            for f in range(2):
                a_arrive(k, f, shard_at(shard_dy, True))
        both = nn_dot(gathered[k, 0], q_mat[0:QUART, :]) + nn_dot(gathered[k, 1], q_mat[QUART:HALF, :])
        halves[k, 0] = both[:, 0:HEAD]
        halves[k, 1] = both[:, HEAD : 2 * HEAD]
        send(halves.at[k, other], halves_in.at[k], h_send.at[k], h_recv.at[k], partner)

    def finish_queries(k):
        arrive(halves_in.at[k], h_recv.at[k])
        values = halves[k, core] + halves_in[k] + qb_ref[...].astype(F32)
        values = rotated(values, cos_ref[k], sin_ref[k]) * (LOG2E / math.sqrt(HEAD))
        queries[0, k] = values.astype(BF16)
        send(queries.at[0, k], queries.at[1, k], q_send.at[k, 0], q_recv.at[k, 0], device(3, 0, 0))
        send(queries.at[0, k], queries.at[2, k], q_send.at[k, 1], q_recv.at[k, 1], device(-3, 0, 0))

    token = lax.broadcasted_iota(jnp.int32, (CHUNK, 1), 0)
    token = (token // PIECE) * SHARD + lax.rem(token, PIECE)
    key_token = lax.broadcasted_iota(jnp.int32, (1, GROUP), 1)

    def attend(k, source, first, last):
        query = queries[source, k]
        query_group = lax.rem(z + (0, 5, 3)[source], 8)
        query_token = query_group * GROUP + k * PIECE + token

        def over(slot, total, top):
            prefix = nt_dot(query, pre_k[slot]) + mask[slot]
            span = nt_dot(query, span_k[slot])
            key_group = lax.rem(z + slot + 7, 8)
            span = jnp.where(key_group * GROUP + key_token <= query_token, span, NEG)
            new_top = jnp.maximum(
                jnp.max(prefix, axis=1, keepdims=True), jnp.max(span, axis=1, keepdims=True)
            )
            if top is not None:
                new_top = jnp.maximum(new_top, top)
            blended = nn_dot(jnp.exp2(prefix - new_top).astype(BF16), pre_v[slot])
            blended = blended + nn_dot(jnp.exp2(span - new_top).astype(BF16), span_v[slot])
            if top is not None:
                blended = blended + total * jnp.exp2(top - new_top)
            return blended, new_top

        state = over(first, None, None)
        return lax.fori_loop(first + 1, last, lambda s, c: over(s, *c), state)

    def attend_own(k):
        total, top = attend(k, 0, 0, 3)
        own_o[k] = total
        own_m[k] = jnp.broadcast_to(top, (CHUNK, HEAD))

    def attend_other(k):
        for i, (source, first) in enumerate(((1, 0), (2, 1))):
            arrive(queries.at[source, k], q_recv.at[k, i])
            total, top = attend(k, source, first, 3)
            part_o[k, i] = total[:, 0:HEAD].astype(BF16)
            part_s[k, i, 0:4, :] = jnp.transpose(jnp.broadcast_to(top, (CHUNK, HEAD)))[0:4, :]
            part_s[k, i, 4:8, :] = jnp.transpose(total[:, HEAD : 2 * HEAD])[0:4, :]
            back = device(-3 if source == 1 else 3, 0, 0)
            send(part_o.at[k, i], part_o_in.at[k, i], p_send.at[k, i, 0], p_recv.at[k, i, 0], back)
            send(part_s.at[k, i], part_s_in.at[k, i], p_send.at[k, i, 1], p_recv.at[k, i, 1], back)

    def combine(k):
        total, low, top = own_o[k][:, 0:HEAD], own_o[k][:, HEAD : 2 * HEAD], own_m[k]
        for i in range(2):
            arrive(part_o_in.at[k, i], p_recv.at[k, i, 0])
            arrive(part_s_in.at[k, i], p_recv.at[k, i, 1])
            their_top = jnp.transpose(jnp.broadcast_to(part_s_in[k, i, 0:1, :], (CHUNK, HEAD)))
            their_low = jnp.transpose(jnp.broadcast_to(part_s_in[k, i, 4:5, :], (CHUNK, HEAD)))
            new_top = jnp.maximum(top, their_top)
            mine, theirs = jnp.exp2(top - new_top), jnp.exp2(their_top - new_top)
            total = total * mine + part_o_in[k, i].astype(F32) * theirs
            low = low * mine + their_low * theirs
            top = new_top
        attended[k, :, own_cols] = (total / low).astype(BF16)
        here = attended.at[k, :, own_cols]
        send(here, here, t_send.at[k], t_recv.at[k], partner)

    first = x * other + y * core
    second = y * other + x * core

    def along(stage, ahead):
        on_x = other if stage == 0 else core
        return device(0, ahead * on_x, ahead * (1 - on_x))

    def product(k, block):
        return nn_dot(attended[k], o_mat[block])

    def attended_arrive(k):
        arrive(attended.at[k, :, pl.ds(pl.multiple_of(other * HEAD, HEAD), HEAD)], t_recv.at[k])

    def stage_one(k):
        for ahead in (2, 1, 3):
            value = product(k, lax.rem(first + ahead, 4)).astype(BF16)
            for b in range(4):
                one_out[k, ahead - 1, b] = value[:, b * 256 : (b + 1) * 256]
            at = (k, ahead - 1)
            send(one_out.at[at], one_in.at[at], one_send.at[at], one_recv.at[at], along(0, ahead))
        value = product(k, first)
        for b in range(4):
            mid[k, b] = value[:, b * 256 : (b + 1) * 256]

    def stage_two(k):
        for i in range(3):
            arrive(one_in.at[k, i], one_recv.at[k, i])
        for ahead in (2, 1, 3, 0):
            b = lax.rem(second + ahead, 4)
            value = mid[k, b]
            for i in range(3):
                value = value + one_in[k, i, b].astype(F32)
            if ahead == 0:
                mid[k, b] = value
            else:
                at = (k, ahead - 1)
                two_out[at] = value.astype(BF16)
                send(two_out.at[at], two_in.at[at], two_send.at[at], two_recv.at[at], along(1, ahead))

    def finish(k):
        value = mid[k, second]
        for i in range(3):
            arrive(two_in.at[k, i], two_recv.at[k, i])
            value = value + two_in[k, i].astype(F32)
        result = value.astype(BF16)
        for i in range(SHARDS):
            at = i * SHARD + k * PIECE
            out_ref[at : at + PIECE, :] = result[i * PIECE : (i + 1) * PIECE, :]

    a_mid(1)
    a_last(0)
    span_forward()
    a_mid(2)
    load_qw.wait()
    arrive(q_mat.at[:, pl.ds(pl.multiple_of(other * HEAD, HEAD), HEAD)], w_recv.at[0])
    project(0)
    a_last(1)
    finish_queries(0)
    a_last(2)
    project(1)
    neighbours_arrive()
    finish_queries(1)
    attend_own(0)
    project(2)
    pltpu.make_async_copy(o_mat.at[:, own_cols, :], o_mat.at[:, own_cols, :], local_sems.at[5]).wait()
    arrive(o_mat.at[:, pl.ds(pl.multiple_of(other * HEAD, HEAD), HEAD), :], w_recv.at[1])
    finish_queries(2)
    attend_other(0)
    attend_own(1)
    attend_other(1)
    attend_own(2)
    combine(0)
    attended_arrive(0)
    stage_one(0)
    attend_other(2)
    combine(1)
    attended_arrive(1)
    stage_one(1)
    stage_two(0)
    combine(2)
    attended_arrive(2)
    stage_one(2)
    stage_two(1)
    finish(0)
    stage_two(2)
    finish(1)
    finish(2)

    for copy in sent:
        copy.wait_send()
    theirs = o_mat.at[:, pl.ds(pl.multiple_of(other * HEAD, HEAD), HEAD), :]
    remote(theirs, theirs, w_send.at[1], w_recv.at[1], partner).wait_send()


def local(
    hidden, norm_gain, q_weight, q_bias, key_weight, key_bias, value_weight, value_bias, o_weight,
    cached_key_rows, cached_value_rows, keep_blocks, kept_counts, span_start,
):
    group = lax.axis_index("ctx")
    token = jnp.arange(CHUNKS * CHUNK, dtype=jnp.int32)
    token = (token % CHUNK // PIECE) * SHARD + token // CHUNK * PIECE + token % PIECE
    positions = span_start[0] + group * GROUP + token
    steps = jnp.arange(HEAD // 2, dtype=F32)
    frequency = 1000000.0 ** (-2.0 * steps / HEAD)
    angles = positions.astype(F32)[:, None] * frequency[None, :]
    cosine, sine = jnp.cos(angles), jnp.sin(angles)
    cosine = jnp.concatenate([cosine, cosine], axis=1).reshape(CHUNKS, CHUNK, HEAD)
    sine = jnp.concatenate([-sine, sine], axis=1).reshape(CHUNKS, CHUNK, HEAD)

    vmem = pl.BlockSpec(memory_space=pltpu.VMEM)
    smem = pl.BlockSpec(memory_space=pltpu.SMEM)
    hbm = pl.BlockSpec(memory_space=pl.ANY)
    dma = pltpu.SemaphoreType.DMA
    kept = jax.ShapeDtypeStruct((KEPT, HEAD), BF16)
    kept_k, kept_v, mask = pl.pallas_call(
        keep_kernel,
        out_shape=(kept, kept, jax.ShapeDtypeStruct((3, 1, KEPT), F32)),
        in_specs=[smem, smem, hbm, hbm],
        out_specs=(vmem, vmem, vmem),
        scratch_shapes=[dma((2, KEEP))],
        name="kept_blocks",
    )(keep_blocks, kept_counts, cached_key_rows, cached_value_rows)
    scratch = [
        pltpu.VMEM((SHARD, WIDTH), BF16),
        pltpu.VMEM((CHUNKS, 2, CHUNK, QUART), BF16),
        pltpu.VMEM((HALF, 2 * HEAD), BF16),
        pltpu.VMEM((WIDTH, 2 * HEAD), BF16),
        pltpu.VMEM((4, 2 * HEAD, 1024), BF16),
        pltpu.VMEM((3, KEPT, HEAD), BF16),
        pltpu.VMEM((3, KEPT, 2 * HEAD), BF16),
        pltpu.VMEM((3, GROUP, HEAD), BF16),
        pltpu.VMEM((3, GROUP, 2 * HEAD), BF16),
        pltpu.VMEM((CHUNKS, 2, CHUNK, HEAD), F32),
        pltpu.VMEM((CHUNKS, CHUNK, HEAD), F32),
        pltpu.VMEM((3, CHUNKS, CHUNK, HEAD), BF16),
        pltpu.VMEM((CHUNKS, 2, CHUNK, HEAD), BF16),
        pltpu.VMEM((CHUNKS, 2, 8, CHUNK), F32),
        pltpu.VMEM((CHUNKS, 2, CHUNK, HEAD), BF16),
        pltpu.VMEM((CHUNKS, 2, 8, CHUNK), F32),
        pltpu.VMEM((CHUNKS, CHUNK, 2 * HEAD), F32),
        pltpu.VMEM((CHUNKS, CHUNK, HEAD), F32),
        pltpu.VMEM((CHUNKS, CHUNK, 2 * HEAD), BF16),
        pltpu.VMEM((CHUNKS, 3, 4, CHUNK, 256), BF16),
        pltpu.VMEM((CHUNKS, 3, 4, CHUNK, 256), BF16),
        pltpu.VMEM((CHUNKS, 4, CHUNK, 256), F32),
        pltpu.VMEM((CHUNKS, 3, CHUNK, 256), BF16),
        pltpu.VMEM((CHUNKS, 3, CHUNK, 256), BF16),
        dma((6,)),
        dma((CHUNKS, 14)), dma((CHUNKS, 2, SHARDS)),
        dma((2,)), dma((2,)),
        dma((2, 2)), dma((2, 3)),
        dma((2, SHARDS)), dma((2, SHARDS)),
        dma((2, 2)), dma((2, 3)),
        dma((CHUNKS,)), dma((CHUNKS,)),
        dma((CHUNKS, 2)), dma((CHUNKS, 2)),
        dma((CHUNKS, 2, 2)), dma((CHUNKS, 2, 2)),
        dma((CHUNKS,)), dma((CHUNKS,)),
        dma((CHUNKS, 3)), dma((CHUNKS, 3)),
        dma((CHUNKS, 3)), dma((CHUNKS, 3)),
    ]
    return pl.pallas_call(
        kernel,
        out_shape=jax.ShapeDtypeStruct((GROUP, 256), BF16),
        in_specs=[vmem, vmem, hbm, vmem, hbm, vmem, hbm, vmem, hbm, hbm, hbm, vmem, vmem, vmem],
        out_specs=vmem,
        scratch_shapes=scratch,
        compiler_params=pltpu.CompilerParams(
            collective_id=0, has_side_effects=True, vmem_limit_bytes=56 * 1024 * 1024
        ),
        name="attention_sublayer",
    )(
        hidden, norm_gain.reshape(1, -1), q_weight, q_bias.reshape(1, -1), key_weight, key_bias.reshape(1, -1),
        value_weight, value_bias.reshape(1, -1), o_weight, kept_k, kept_v, mask, cosine, sine,
    )


def solution(mesh):
    in_specs = (
        P(("ctx", "row"), None),
        P(),
        P(None, ("head", "row")),
        P(("head", "row")),
        P(None, "head"),
        P("head"),
        P(None, "head"),
        P("head"),
        P(("head", "row"), None),
        P("ctx", "head"),
        P("ctx", "head"),
        P("ctx", None),
        P(),
        P(),
    )
    out_specs = P("ctx", ("head", "row"))
    return jax.shard_map(local, mesh=mesh, in_specs=in_specs, out_specs=out_specs, check_vma=False)
```

```python
import math

import jax
import jax.numpy as jnp
import numpy as np
from jax import lax
from jax.experimental import pallas as pl
from jax.experimental.pallas import tpu as pltpu
from jax.sharding import PartitionSpec as P

MESH = pl.DeviceIdType.MESH
F32 = jnp.float32
BF16 = jnp.bfloat16

N_CTX = 8
WIDTH = 8192
HALF = 4096
QUART = 2048
HEAD = 128
BLOCK = 128
KEEP = 8
SHARDS = 8
SHARD = 48
CHUNKS = 3
PIECE = 16
CHUNK = SHARDS * PIECE
GROUP = SHARDS * SHARD
KEPT = KEEP * BLOCK
NEG = -1e30
LOG2E = math.log2(math.e)


def nt_dot(a, b):
    return lax.dot_general(a, b, (((1,), (1,)), ((), ())), preferred_element_type=F32)


def nn_dot(a, b):
    return lax.dot_general(a, b, (((1,), (0,)), ((), ())), preferred_element_type=F32)


def kernel(
    hidden_ref, gain_ref, qw_ref, qb_ref, kw_ref, kb_ref, vw_ref, vb_ref, ow_ref, ck_ref, cv_ref,
    blocks_ref, counts_ref, start_ref, freq_ref,
    out_ref,
    normed, gathered, q_mat, kv_mat, o_mat, cache_k, cache_v,
    pre_k, pre_v, span_k, span_v, mask, cos_ref, sin_ref,
    halves, halves_in, queries, part_o, part_s, part_o_in, part_s_in,
    own_o, own_m, attended, one_out, one_in, mid, two_out, two_in,
    local_sems, a_send, a_recv, w_send, w_recv, pre_send, pre_recv, row_send, row_recv, span_send, span_recv,
    h_send, h_recv, q_send, q_recv, p_send, p_recv, t_send, t_recv, one_send, one_recv, two_send, two_recv,
):
    z = lax.axis_index("ctx")
    head = lax.axis_index("head")
    row = lax.axis_index("row")
    core = lax.rem(head, 2)
    x_lo = row // 4
    y = lax.rem(row, 4)
    x = 2 * (head // 2) + x_lo
    other = 1 - core

    def device(dz, dx, dy, dc=None):
        xx = lax.rem(x + dx + 4, 4)
        yy = lax.rem(y + dy + 4, 4)
        cc = core if dc is None else dc
        return (lax.rem(z + dz + 8, 8), 2 * (xx // 2) + cc, 4 * lax.rem(xx, 2) + yy)

    def row_peer(step):
        return (z, head, lax.rem(row + step, SHARDS))

    partner = (z, 2 * (head // 2) + other, row)

    def remote(src, dst, send, recv, to):
        return pltpu.make_async_remote_copy(
            src_ref=src, dst_ref=dst, send_sem=send, recv_sem=recv, device_id=to, device_id_type=MESH
        )

    sent = []

    def send(src, dst, send_sem, recv_sem, to):
        copy = remote(src, dst, send_sem, recv_sem, to)
        copy.start()
        sent.append(copy)

    def arrive(dst, recv_sem):
        remote(dst, dst, recv_sem, recv_sem, partner).wait_recv()

    def load(src, dst, i):
        copy = pltpu.make_async_copy(src, dst, local_sems.at[i])
        copy.start()
        return copy

    load_k = load(ck_ref, cache_k, 0)
    load_v = load(cv_ref, cache_v, 1)
    load_kw = load(kw_ref, kv_mat.at[:, 0:HEAD], 2)
    load_vw = load(vw_ref, kv_mat.at[:, HEAD : 2 * HEAD], 3)
    own_cols = pl.ds(pl.multiple_of(core * HEAD, HEAD), HEAD)
    load_qw = load(qw_ref.at[pl.ds(pl.multiple_of(core * HALF, HALF), HALF), :], q_mat.at[:, own_cols], 4)

    def column(cc, first, second):
        xx = first * (1 - cc) + second * cc
        yy = second * (1 - cc) + first * cc
        return pl.multiple_of((2 * (xx // 2) + cc) * 2048 + (4 * lax.rem(xx, 2) + yy) * 256, 256)

    for b1 in range(4):
        for b2 in range(4):
            pltpu.make_async_copy(
                ow_ref.at[:, pl.ds(column(core, b1, b2), 256)],
                o_mat.at[b1, own_cols, pl.ds(b2 * 256, 256)],
                local_sems.at[5],
            ).start()

    barrier = pltpu.get_barrier_semaphore()
    partners = [partner]
    partners += [device(0, 1, 0), device(0, -1, 0), device(0, 2, 0)]
    partners += [row_peer(s) for s in range(1, SHARDS)]
    partners += [device(dz, 0, 0) for dz in (1, -1, 3, -3)]
    for to in partners:
        pl.semaphore_signal(barrier, inc=1, device_id=to, device_id_type=MESH)
    pl.semaphore_wait(barrier, len(partners))

    def rows_of(shard):
        return pl.ds(pl.multiple_of(shard * PIECE, PIECE), PIECE)

    def normalise(k):
        rows = slice(k * PIECE, (k + 1) * PIECE)
        total = jnp.zeros((PIECE, 1), F32)
        for i in range(8):
            part = hidden_ref[rows, i * 1024 : (i + 1) * 1024].astype(F32)
            total = total + jnp.sum(part * part, axis=1, keepdims=True)
        factor = lax.rsqrt(total / WIDTH + 1e-6)
        for i in range(8):
            cols = slice(i * 1024, (i + 1) * 1024)
            part = hidden_ref[rows, cols].astype(F32) * factor * gain_ref[cols].astype(F32).reshape(1, 1024)
            normed[rows, cols] = part.astype(BF16)
        for f in range(2):
            cols = pl.ds(pl.multiple_of(core * HALF + f * QUART, QUART), QUART)
            gathered[k, f, rows_of(row), :] = normed[rows, cols]

    y_up, y_down = device(0, 0, 1), device(0, 0, -1)
    x_up, x_down = device(0, 1, 0), device(0, -1, 0)
    a_count = [0, 0, 0]

    def forward(k, f, shard, to):
        piece = gathered.at[k, f, rows_of(shard), :]
        send(piece, piece, a_send.at[k, a_count[k]], a_recv.at[k, f, shard], to)
        a_count[k] += 1

    def shard_at(dy, flip=False):
        xl = 1 - x_lo if flip else x_lo
        return 4 * xl + lax.rem(y + dy + 4, 4)

    def a_arrive(k, f, shard):
        arrive(gathered.at[k, f, rows_of(shard), :], a_recv.at[k, f, shard])

    def a_start(k):
        forward(k, 0, row, x_up)
        forward(k, 0, row, y_up)
        forward(k, 1, row, x_down)
        forward(k, 1, row, y_down)
        forward(k, 1, row, y_up)
        forward(k, 0, row, y_down)

    def a_mid(k):
        below, above = shard_at(-1), shard_at(1)
        a_arrive(k, 0, below)
        forward(k, 0, below, y_up)
        forward(k, 0, below, x_up)
        a_arrive(k, 1, above)
        forward(k, 1, above, y_down)
        forward(k, 1, above, x_down)
        a_arrive(k, 1, below)
        forward(k, 1, below, x_down)
        a_arrive(k, 0, above)
        forward(k, 0, above, x_up)

    def a_last(k):
        far = shard_at(2)
        a_arrive(k, 0, far)
        forward(k, 0, far, x_up)
        a_arrive(k, 1, far)
        forward(k, 1, far, x_down)

    normalise(0)
    a_start(0)
    normalise(1)
    a_start(1)
    normalise(2)

    send(
        qw_ref.at[pl.ds(pl.multiple_of(other * HALF, HALF), HALF), :],
        q_mat.at[:, own_cols], w_send.at[0], w_recv.at[0], partner,
    )
    load_k.wait()
    load_v.wait()
    for j in range(KEEP):
        pre_k[1, j * BLOCK : (j + 1) * BLOCK, :] = cache_k[blocks_ref[0, j]]
        pre_v[1, j * BLOCK : (j + 1) * BLOCK, 0:HEAD] = cache_v[blocks_ref[0, j]]
    z_up, z_down = device(1, 0, 0), device(-1, 0, 0)
    left = pl.ds(0, HEAD)
    for s in range(3):
        pre_v[s, :, HEAD : 2 * HEAD] = jnp.ones((KEPT, HEAD), BF16)
        span_v[s, :, HEAD : 2 * HEAD] = jnp.ones((GROUP, HEAD), BF16)
        live = counts_ref[lax.rem(z + s + 7, N_CTX)]
        slot_index = lax.broadcasted_iota(jnp.int32, (1, KEPT), 1) // BLOCK
        mask[s] = jnp.where(slot_index < live, 0.0, NEG).astype(F32)

    token = lax.broadcasted_iota(jnp.int32, (CHUNK, 1), 0)
    token = (token // PIECE) * SHARD + lax.rem(token, PIECE)
    sign = jnp.where(lax.broadcasted_iota(jnp.int32, (1, HEAD), 1) < HEAD // 2, -1.0, 1.0)

    def angles_of(k):
        positions = (start_ref[0] + z * GROUP + k * PIECE + token).astype(F32)
        angles = positions * freq_ref[...]
        cos_ref[k] = jnp.cos(angles)
        sin_ref[k] = jnp.sin(angles) * sign

    for k in range(CHUNKS):
        angles_of(k)

    def rotated(values, cosine, sine):
        return values * cosine + pltpu.roll(values, HEAD // 2, 1) * sine

    load_kw.wait()
    load_vw.wait()

    def kv_step(i, total):
        at = pl.ds(pl.multiple_of(i * 1024, 1024), 1024)
        return total + nn_dot(normed[:, at], kv_mat[at, :])

    def span_rows(shard):
        return pl.ds(pl.multiple_of(shard * SHARD, SHARD), SHARD)

    pair = lax.fori_loop(0, 4, kv_step, jnp.zeros((SHARD, 2 * HEAD), F32))
    a_mid(0)
    a_start(2)
    for i, (slot, to) in enumerate(((0, z_up), (2, z_down))):
        send(pre_k.at[1], pre_k.at[slot], pre_send.at[0, i], pre_recv.at[0, slot], to)
        send(pre_v.at[1, :, left], pre_v.at[slot, :, left], pre_send.at[1, i], pre_recv.at[1, slot], to)

    pair = lax.fori_loop(4, 8, kv_step, pair)
    key_part = pair[:, 0:HEAD] + kb_ref[...].astype(F32).reshape(1, HEAD)
    value_part = pair[:, HEAD : 2 * HEAD] + vb_ref[...].astype(F32).reshape(1, HEAD)
    own_cos = jnp.concatenate([cos_ref[k, rows_of(row), :] for k in range(CHUNKS)], axis=0)
    own_sin = jnp.concatenate([sin_ref[k, rows_of(row), :] for k in range(CHUNKS)], axis=0)

    span_k[1, span_rows(row), :] = rotated(key_part, own_cos, own_sin).astype(BF16)
    span_v[1, span_rows(row), 0:HEAD] = value_part.astype(BF16)
    for s in range(1, SHARDS):
        here = span_k.at[1, span_rows(row), :]
        send(here, here, row_send.at[0, s], row_recv.at[0, row], row_peer(s))
        here = span_v.at[1, span_rows(row), left]
        send(here, here, row_send.at[1, s], row_recv.at[1, row], row_peer(s))

    def span_forward():
        for s in range(1, SHARDS):
            peer = lax.rem(row + s, SHARDS)
            arrive(span_k.at[1, span_rows(peer), :], row_recv.at[0, peer])
            arrive(span_v.at[1, span_rows(peer), left], row_recv.at[1, peer])
        for i, (slot, to) in enumerate(((0, z_up), (2, z_down))):
            send(span_k.at[1], span_k.at[slot], span_send.at[0, i], span_recv.at[0, slot], to)
            send(span_v.at[1, :, left], span_v.at[slot, :, left], span_send.at[1, i], span_recv.at[1, slot], to)

    def neighbours_arrive():
        for slot in (0, 2):
            arrive(pre_k.at[slot], pre_recv.at[0, slot])
            arrive(pre_v.at[slot, :, left], pre_recv.at[1, slot])
            arrive(span_k.at[slot], span_recv.at[0, slot])
            arrive(span_v.at[slot, :, left], span_recv.at[1, slot])

    def project(k):
        for shard_dy in range(4):
            for f in range(2):
                a_arrive(k, f, shard_at(shard_dy, True))
        both = nn_dot(gathered[k, 0], q_mat[0:QUART, :]) + nn_dot(gathered[k, 1], q_mat[QUART:HALF, :])
        halves[k, 0] = both[:, 0:HEAD]
        halves[k, 1] = both[:, HEAD : 2 * HEAD]
        send(halves.at[k, other], halves_in.at[k], h_send.at[k], h_recv.at[k], partner)

    def finish_queries(k):
        arrive(halves_in.at[k], h_recv.at[k])
        values = halves[k, core] + halves_in[k] + qb_ref[...].astype(F32).reshape(1, HEAD)
        values = rotated(values, cos_ref[k], sin_ref[k]) * (LOG2E / math.sqrt(HEAD))
        queries[0, k] = values.astype(BF16)
        send(queries.at[0, k], queries.at[1, k], q_send.at[k, 0], q_recv.at[k, 0], device(3, 0, 0))
        send(queries.at[0, k], queries.at[2, k], q_send.at[k, 1], q_recv.at[k, 1], device(-3, 0, 0))

    key_token = lax.broadcasted_iota(jnp.int32, (1, GROUP), 1)

    def attend(k, source, first, last):
        query = queries[source, k]
        query_group = lax.rem(z + (0, 5, 3)[source], 8)
        query_token = query_group * GROUP + k * PIECE + token

        def over(slot, total, top):
            prefix = nt_dot(query, pre_k[slot]) + mask[slot]
            span = nt_dot(query, span_k[slot])
            key_group = lax.rem(z + slot + 7, 8)
            span = jnp.where(key_group * GROUP + key_token <= query_token, span, NEG)
            new_top = jnp.maximum(
                jnp.max(prefix, axis=1, keepdims=True), jnp.max(span, axis=1, keepdims=True)
            )
            if top is not None:
                new_top = jnp.maximum(new_top, top)
            blended = nn_dot(jnp.exp2(prefix - new_top).astype(BF16), pre_v[slot])
            blended = blended + nn_dot(jnp.exp2(span - new_top).astype(BF16), span_v[slot])
            if top is not None:
                blended = blended + total * jnp.exp2(top - new_top)
            return blended, new_top

        state = over(first, None, None)
        return lax.fori_loop(first + 1, last, lambda s, c: over(s, *c), state)

    def attend_own(k):
        total, top = attend(k, 0, 0, 3)
        own_o[k] = total
        own_m[k] = jnp.broadcast_to(top, (CHUNK, HEAD))

    def attend_other(k):
        for i, (source, first) in enumerate(((1, 0), (2, 1))):
            arrive(queries.at[source, k], q_recv.at[k, i])
            total, top = attend(k, source, first, 3)
            part_o[k, i] = total[:, 0:HEAD].astype(BF16)
            part_s[k, i, 0:4, :] = jnp.transpose(jnp.broadcast_to(top, (CHUNK, HEAD)))[0:4, :]
            part_s[k, i, 4:8, :] = jnp.transpose(total[:, HEAD : 2 * HEAD])[0:4, :]
            back = device(-3 if source == 1 else 3, 0, 0)
            send(part_o.at[k, i], part_o_in.at[k, i], p_send.at[k, i, 0], p_recv.at[k, i, 0], back)
            send(part_s.at[k, i], part_s_in.at[k, i], p_send.at[k, i, 1], p_recv.at[k, i, 1], back)

    def combine(k):
        total, low, top = own_o[k][:, 0:HEAD], own_o[k][:, HEAD : 2 * HEAD], own_m[k]
        for i in range(2):
            arrive(part_o_in.at[k, i], p_recv.at[k, i, 0])
            arrive(part_s_in.at[k, i], p_recv.at[k, i, 1])
            their_top = jnp.transpose(jnp.broadcast_to(part_s_in[k, i, 0:1, :], (CHUNK, HEAD)))
            their_low = jnp.transpose(jnp.broadcast_to(part_s_in[k, i, 4:5, :], (CHUNK, HEAD)))
            new_top = jnp.maximum(top, their_top)
            mine, theirs = jnp.exp2(top - new_top), jnp.exp2(their_top - new_top)
            total = total * mine + part_o_in[k, i].astype(F32) * theirs
            low = low * mine + their_low * theirs
            top = new_top
        attended[k, :, own_cols] = (total / low).astype(BF16)
        here = attended.at[k, :, own_cols]
        send(here, here, t_send.at[k], t_recv.at[k], partner)

    first = x * other + y * core
    second = y * other + x * core

    def along(stage, ahead):
        on_x = other if stage == 0 else core
        return device(0, ahead * on_x, ahead * (1 - on_x))

    def product(k, block):
        return nn_dot(attended[k], o_mat[block])

    def attended_arrive(k):
        arrive(attended.at[k, :, pl.ds(pl.multiple_of(other * HEAD, HEAD), HEAD)], t_recv.at[k])

    def stage_one(k):
        for ahead in (2, 1, 3):
            value = product(k, lax.rem(first + ahead, 4)).astype(BF16)
            for b in range(4):
                one_out[k, ahead - 1, b] = value[:, b * 256 : (b + 1) * 256]
            at = (k, ahead - 1)
            send(one_out.at[at], one_in.at[at], one_send.at[at], one_recv.at[at], along(0, ahead))
        value = product(k, first)
        for b in range(4):
            mid[k, b] = value[:, b * 256 : (b + 1) * 256]

    def stage_two(k):
        for i in range(3):
            arrive(one_in.at[k, i], one_recv.at[k, i])
        for ahead in (2, 1, 3, 0):
            b = lax.rem(second + ahead, 4)
            value = mid[k, b]
            for i in range(3):
                value = value + one_in[k, i, b].astype(F32)
            if ahead == 0:
                mid[k, b] = value
            else:
                at = (k, ahead - 1)
                two_out[at] = value.astype(BF16)
                send(two_out.at[at], two_in.at[at], two_send.at[at], two_recv.at[at], along(1, ahead))

    def finish(k):
        value = mid[k, second]
        for i in range(3):
            arrive(two_in.at[k, i], two_recv.at[k, i])
            value = value + two_in[k, i].astype(F32)
        result = value.astype(BF16)
        for i in range(SHARDS):
            at = i * SHARD + k * PIECE
            out_ref[at : at + PIECE, :] = result[i * PIECE : (i + 1) * PIECE, :]

    a_mid(1)
    a_last(0)
    span_forward()
    a_mid(2)
    load_qw.wait()
    arrive(q_mat.at[:, pl.ds(pl.multiple_of(other * HEAD, HEAD), HEAD)], w_recv.at[0])
    project(0)
    a_last(1)
    finish_queries(0)
    a_last(2)
    for b1 in range(4):
        for b2 in range(4):
            remote(
                ow_ref.at[:, pl.ds(column(other, b1, b2), 256)],
                o_mat.at[b1, own_cols, pl.ds(b2 * 256, 256)],
                w_send.at[1], w_recv.at[1], partner,
            ).start()

    project(1)
    neighbours_arrive()
    finish_queries(1)
    attend_own(0)
    project(2)
    pltpu.make_async_copy(o_mat.at[:, own_cols, :], o_mat.at[:, own_cols, :], local_sems.at[5]).wait()
    arrive(o_mat.at[:, pl.ds(pl.multiple_of(other * HEAD, HEAD), HEAD), :], w_recv.at[1])
    finish_queries(2)
    attend_other(0)
    attend_own(1)
    attend_other(1)
    attend_own(2)
    combine(0)
    attended_arrive(0)
    stage_one(0)
    attend_other(2)
    combine(1)
    attended_arrive(1)
    stage_one(1)
    stage_two(0)
    combine(2)
    attended_arrive(2)
    stage_one(2)
    stage_two(1)
    finish(0)
    stage_two(2)
    finish(1)
    finish(2)

    for copy in sent:
        copy.wait_send()
    theirs = o_mat.at[:, pl.ds(pl.multiple_of(other * HEAD, HEAD), HEAD), :]
    remote(theirs, theirs, w_send.at[1], w_recv.at[1], partner).wait_send()


def local(
    hidden, norm_gain, q_weight, q_bias, key_weight, key_bias, value_weight, value_bias, o_weight,
    cached_key_rows, cached_value_rows, keep_blocks, kept_counts, span_start,
):
    steps = np.arange(HEAD // 2, dtype=np.float64)
    frequency = (1000000.0 ** (-2.0 * steps / HEAD)).astype(np.float32)
    frequency = np.concatenate([frequency, frequency])[None, :]

    vmem = pl.BlockSpec(memory_space=pltpu.VMEM)
    smem = pl.BlockSpec(memory_space=pltpu.SMEM)
    hbm = pl.BlockSpec(memory_space=pl.ANY)
    dma = pltpu.SemaphoreType.DMA
    scratch = [
        pltpu.VMEM((SHARD, WIDTH), BF16),
        pltpu.VMEM((CHUNKS, 2, CHUNK, QUART), BF16),
        pltpu.VMEM((HALF, 2 * HEAD), BF16),
        pltpu.VMEM((WIDTH, 2 * HEAD), BF16),
        pltpu.VMEM((4, 2 * HEAD, 1024), BF16),
        pltpu.VMEM((32, BLOCK, HEAD), BF16),
        pltpu.VMEM((32, BLOCK, HEAD), BF16),
        pltpu.VMEM((3, KEPT, HEAD), BF16),
        pltpu.VMEM((3, KEPT, 2 * HEAD), BF16),
        pltpu.VMEM((3, GROUP, HEAD), BF16),
        pltpu.VMEM((3, GROUP, 2 * HEAD), BF16),
        pltpu.VMEM((3, 1, KEPT), F32),
        pltpu.VMEM((CHUNKS, CHUNK, HEAD), F32),
        pltpu.VMEM((CHUNKS, CHUNK, HEAD), F32),
        pltpu.VMEM((CHUNKS, 2, CHUNK, HEAD), F32),
        pltpu.VMEM((CHUNKS, CHUNK, HEAD), F32),
        pltpu.VMEM((3, CHUNKS, CHUNK, HEAD), BF16),
        pltpu.VMEM((CHUNKS, 2, CHUNK, HEAD), BF16),
        pltpu.VMEM((CHUNKS, 2, 8, CHUNK), F32),
        pltpu.VMEM((CHUNKS, 2, CHUNK, HEAD), BF16),
        pltpu.VMEM((CHUNKS, 2, 8, CHUNK), F32),
        pltpu.VMEM((CHUNKS, CHUNK, 2 * HEAD), F32),
        pltpu.VMEM((CHUNKS, CHUNK, HEAD), F32),
        pltpu.VMEM((CHUNKS, CHUNK, 2 * HEAD), BF16),
        pltpu.VMEM((CHUNKS, 3, 4, CHUNK, 256), BF16),
        pltpu.VMEM((CHUNKS, 3, 4, CHUNK, 256), BF16),
        pltpu.VMEM((CHUNKS, 4, CHUNK, 256), F32),
        pltpu.VMEM((CHUNKS, 3, CHUNK, 256), BF16),
        pltpu.VMEM((CHUNKS, 3, CHUNK, 256), BF16),
        dma((6,)),
        dma((CHUNKS, 14)), dma((CHUNKS, 2, SHARDS)),
        dma((2,)), dma((2,)),
        dma((2, 2)), dma((2, 3)),
        dma((2, SHARDS)), dma((2, SHARDS)),
        dma((2, 2)), dma((2, 3)),
        dma((CHUNKS,)), dma((CHUNKS,)),
        dma((CHUNKS, 2)), dma((CHUNKS, 2)),
        dma((CHUNKS, 2, 2)), dma((CHUNKS, 2, 2)),
        dma((CHUNKS,)), dma((CHUNKS,)),
        dma((CHUNKS, 3)), dma((CHUNKS, 3)),
        dma((CHUNKS, 3)), dma((CHUNKS, 3)),
    ]
    return pl.pallas_call(
        kernel,
        out_shape=jax.ShapeDtypeStruct((GROUP, 256), BF16),
        in_specs=[vmem, vmem, hbm, vmem, hbm, vmem, hbm, vmem, hbm, hbm, hbm, smem, smem, smem, vmem],
        out_specs=vmem,
        scratch_shapes=scratch,
        compiler_params=pltpu.CompilerParams(
            collective_id=0, has_side_effects=True, vmem_limit_bytes=56 * 1024 * 1024
        ),
        name="attention_sublayer",
    )(
        hidden, norm_gain, q_weight, q_bias, key_weight, key_bias, value_weight, value_bias, o_weight,
        cached_key_rows.reshape(32, BLOCK, HEAD), cached_value_rows.reshape(32, BLOCK, HEAD),
        keep_blocks, kept_counts, span_start, jnp.asarray(frequency),
    )


def solution(mesh):
    in_specs = (
        P(("ctx", "row"), None),
        P(),
        P(None, ("head", "row")),
        P(("head", "row")),
        P(None, "head"),
        P("head"),
        P(None, "head"),
        P("head"),
        P(("head", "row"), None),
        P("ctx", "head"),
        P("ctx", "head"),
        P("ctx", None),
        P(),
        P(),
    )
    out_specs = P("ctx", ("head", "row"))
    return jax.shard_map(local, mesh=mesh, in_specs=in_specs, out_specs=out_specs, check_vma=False)
```

```python
import math

import jax
import jax.numpy as jnp
import numpy as np
from jax import lax
from jax.experimental import pallas as pl
from jax.experimental.pallas import tpu as pltpu
from jax.sharding import PartitionSpec as P

MESH = pl.DeviceIdType.MESH
F32 = jnp.float32
BF16 = jnp.bfloat16

N_CTX = 8
WIDTH = 8192
HALF = 4096
QUART = 2048
HEAD = 128
BLOCK = 128
KEEP = 8
SHARDS = 8
SHARD = 48
CHUNKS = 3
PIECE = 16
CHUNK = SHARDS * PIECE
GROUP = SHARDS * SHARD
KEPT = KEEP * BLOCK
NEG = -1e30
LOG2E = math.log2(math.e)


def nt_dot(a, b):
    return lax.dot_general(a, b, (((1,), (1,)), ((), ())), preferred_element_type=F32)


def nn_dot(a, b):
    return lax.dot_general(a, b, (((1,), (0,)), ((), ())), preferred_element_type=F32)


def kernel(
    hidden_ref, gain_ref, qw_ref, qb_ref, kw_ref, kb_ref, vw_ref, vb_ref, ow_ref, ck_ref, cv_ref,
    blocks_ref, counts_ref, start_ref, freq_ref,
    out_ref,
    normed, gathered, q_mat, kv_mat, o_mat, cache_k, cache_v,
    pre_k, pre_v, span_k, span_v, mask, cos_ref, sin_ref,
    halves, halves_in, queries, part_o, part_s, part_o_in, part_s_in,
    own_o, own_m, own_head, attended, one_out, one_in, mid,
    local_sems, a_send, a_recv, w_send, w_recv, o_recv, pre_send, pre_recv, row_send, row_recv, span_send, span_recv,
    h_send, h_recv, q_send, q_recv, p_send, p_recv, t_send, t_recv, one_send, one_recv,
):
    z = lax.axis_index("ctx")
    head = lax.axis_index("head")
    row = lax.axis_index("row")
    core = lax.rem(head, 2)
    x_lo = row // 4
    y = lax.rem(row, 4)
    x = 2 * (head // 2) + x_lo
    other = 1 - core

    def device(dz, dx, dy, dc=None):
        xx = lax.rem(x + dx + 4, 4)
        yy = lax.rem(y + dy + 4, 4)
        cc = core if dc is None else dc
        return (lax.rem(z + dz + 8, 8), 2 * (xx // 2) + cc, 4 * lax.rem(xx, 2) + yy)

    def row_peer(step):
        return (z, head, lax.rem(row + step, SHARDS))

    partner = (z, 2 * (head // 2) + other, row)

    def remote(src, dst, send, recv, to):
        return pltpu.make_async_remote_copy(
            src_ref=src, dst_ref=dst, send_sem=send, recv_sem=recv, device_id=to, device_id_type=MESH
        )

    sent = []

    def send(src, dst, send_sem, recv_sem, to):
        copy = remote(src, dst, send_sem, recv_sem, to)
        copy.start()
        sent.append(copy)

    def arrive(dst, recv_sem):
        remote(dst, dst, recv_sem, recv_sem, partner).wait_recv()

    def load(src, dst, i):
        copy = pltpu.make_async_copy(src, dst, local_sems.at[i])
        copy.start()
        return copy

    load_k = load(ck_ref, cache_k, 0)
    load_v = load(cv_ref, cache_v, 1)
    load_kw = load(kw_ref, kv_mat.at[:, 0:HEAD], 2)
    load_vw = load(vw_ref, kv_mat.at[:, HEAD : 2 * HEAD], 3)
    own_cols = pl.ds(pl.multiple_of(core * HEAD, HEAD), HEAD)
    load_qw = load(qw_ref.at[pl.ds(pl.multiple_of(core * HALF, HALF), HALF), :], q_mat.at[:, own_cols], 4)

    def gather_place(cc):
        return y * (1 - cc) + x * cc

    def columns(cc, summed, place):
        xx = summed * (1 - cc) + place * cc
        yy = place * (1 - cc) + summed * cc
        return pl.ds(pl.multiple_of((2 * (xx // 2) + cc) * 2048 + (4 * lax.rem(xx, 2) + yy) * 256, 256), 256)

    def head_slot(cc):
        return 2 * gather_place(cc) + core

    def slot_of(index):
        return pl.ds(pl.multiple_of(index * HEAD, HEAD), HEAD)

    for q in range(4):
        pltpu.make_async_copy(
            ow_ref.at[:, columns(core, q, gather_place(core))],
            o_mat.at[slot_of(head_slot(core)), pl.ds(q * 256, 256)],
            local_sems.at[5],
        ).start()

    barrier = pltpu.get_barrier_semaphore()
    partners = [partner]
    partners += [device(0, s, 0, c) for s in range(1, 4) for c in range(2)]
    partners += [device(0, 0, s, c) for s in range(1, 4) for c in range(2)]
    beside = 4 * (1 - x_lo)
    partners += [(z, head, beside + lax.rem(y + s, 4)) for s in range(1, 4)]
    partners += [device(dz, 0, 0) for dz in (1, -1, 3, -3)]
    for to in partners:
        pl.semaphore_signal(barrier, inc=1, device_id=to, device_id_type=MESH)
    pl.semaphore_wait(barrier, len(partners))

    def rows_of(shard):
        return pl.ds(pl.multiple_of(shard * PIECE, PIECE), PIECE)

    def normalise(k):
        rows = slice(k * PIECE, (k + 1) * PIECE)
        total = jnp.zeros((PIECE, 1), F32)
        for i in range(8):
            part = hidden_ref[rows, i * 1024 : (i + 1) * 1024].astype(F32)
            total = total + jnp.sum(part * part, axis=1, keepdims=True)
        factor = lax.rsqrt(total / WIDTH + 1e-6)
        for i in range(8):
            cols = slice(i * 1024, (i + 1) * 1024)
            part = hidden_ref[rows, cols].astype(F32) * factor * gain_ref[cols].astype(F32).reshape(1, 1024)
            normed[rows, cols] = part.astype(BF16)
        for f in range(2):
            cols = pl.ds(pl.multiple_of(core * HALF + f * QUART, QUART), QUART)
            gathered[k, f, rows_of(row), :] = normed[rows, cols]

    y_up, y_down = device(0, 0, 1), device(0, 0, -1)
    x_up, x_down = device(0, 1, 0), device(0, -1, 0)
    a_count = [0, 0, 0]

    def forward(k, f, shard, to):
        piece = gathered.at[k, f, rows_of(shard), :]
        send(piece, piece, a_send.at[k, a_count[k]], a_recv.at[k, f, shard], to)
        a_count[k] += 1

    def shard_at(dy, flip=False):
        xl = 1 - x_lo if flip else x_lo
        return 4 * xl + lax.rem(y + dy + 4, 4)

    def a_arrive(k, f, shard):
        arrive(gathered.at[k, f, rows_of(shard), :], a_recv.at[k, f, shard])

    def a_start(k):
        forward(k, 0, row, x_up)
        forward(k, 0, row, y_up)
        forward(k, 1, row, x_down)
        forward(k, 1, row, y_down)
        forward(k, 1, row, y_up)
        forward(k, 0, row, y_down)

    def a_mid(k):
        below, above = shard_at(-1), shard_at(1)
        a_arrive(k, 0, below)
        forward(k, 0, below, y_up)
        forward(k, 0, below, x_up)
        a_arrive(k, 1, above)
        forward(k, 1, above, y_down)
        forward(k, 1, above, x_down)
        a_arrive(k, 1, below)
        forward(k, 1, below, x_down)
        a_arrive(k, 0, above)
        forward(k, 0, above, x_up)

    def a_last(k):
        far = shard_at(2)
        a_arrive(k, 0, far)
        forward(k, 0, far, x_up)
        a_arrive(k, 1, far)
        forward(k, 1, far, x_down)

    normalise(0)
    a_start(0)
    normalise(1)
    a_start(1)
    normalise(2)

    send(
        qw_ref.at[pl.ds(pl.multiple_of(other * HALF, HALF), HALF), :],
        q_mat.at[:, own_cols], w_send.at[0], w_recv.at[0], partner,
    )
    load_k.wait()
    load_v.wait()
    for j in range(KEEP):
        pre_k[1, j * BLOCK : (j + 1) * BLOCK, :] = cache_k[blocks_ref[0, j]]
        pre_v[1, j * BLOCK : (j + 1) * BLOCK, 0:HEAD] = cache_v[blocks_ref[0, j]]
    z_up, z_down = device(1, 0, 0), device(-1, 0, 0)
    left = pl.ds(0, HEAD)
    for s in range(3):
        pre_v[s, :, HEAD : 2 * HEAD] = jnp.ones((KEPT, HEAD), BF16)
        span_v[s, :, HEAD : 2 * HEAD] = jnp.ones((GROUP, HEAD), BF16)
        live = counts_ref[lax.rem(z + s + 7, N_CTX)]
        slot_index = lax.broadcasted_iota(jnp.int32, (1, KEPT), 1) // BLOCK
        mask[s] = jnp.where(slot_index < live, 0.0, NEG).astype(F32)

    token = lax.broadcasted_iota(jnp.int32, (CHUNK, 1), 0)
    token = (token // PIECE) * SHARD + lax.rem(token, PIECE)
    sign = jnp.where(lax.broadcasted_iota(jnp.int32, (1, HEAD), 1) < HEAD // 2, -1.0, 1.0)

    def angles_of(k):
        positions = (start_ref[0] + z * GROUP + k * PIECE + token).astype(F32)
        angles = positions * freq_ref[...]
        cos_ref[k] = jnp.cos(angles)
        sin_ref[k] = jnp.sin(angles) * sign

    for k in range(CHUNKS):
        angles_of(k)

    def rotated(values, cosine, sine):
        return values * cosine + pltpu.roll(values, HEAD // 2, 1) * sine

    load_kw.wait()
    load_vw.wait()

    def kv_step(i, total):
        at = pl.ds(pl.multiple_of(i * 1024, 1024), 1024)
        return total + nn_dot(normed[:, at], kv_mat[at, :])

    def span_rows(shard):
        return pl.ds(pl.multiple_of(shard * SHARD, SHARD), SHARD)

    pair = lax.fori_loop(0, 4, kv_step, jnp.zeros((SHARD, 2 * HEAD), F32))
    a_mid(0)
    a_start(2)
    for i, (slot, to) in enumerate(((0, z_up), (2, z_down))):
        send(pre_k.at[1], pre_k.at[slot], pre_send.at[0, i], pre_recv.at[0, slot], to)
        send(pre_v.at[1, :, left], pre_v.at[slot, :, left], pre_send.at[1, i], pre_recv.at[1, slot], to)

    pair = lax.fori_loop(4, 8, kv_step, pair)
    key_part = pair[:, 0:HEAD] + kb_ref[...].astype(F32).reshape(1, HEAD)
    value_part = pair[:, HEAD : 2 * HEAD] + vb_ref[...].astype(F32).reshape(1, HEAD)
    own_cos = jnp.concatenate([cos_ref[k, rows_of(row), :] for k in range(CHUNKS)], axis=0)
    own_sin = jnp.concatenate([sin_ref[k, rows_of(row), :] for k in range(CHUNKS)], axis=0)

    span_k[1, span_rows(row), :] = rotated(key_part, own_cos, own_sin).astype(BF16)
    span_v[1, span_rows(row), 0:HEAD] = value_part.astype(BF16)
    for s in range(1, SHARDS):
        here = span_k.at[1, span_rows(row), :]
        send(here, here, row_send.at[0, s], row_recv.at[0, row], row_peer(s))
        here = span_v.at[1, span_rows(row), left]
        send(here, here, row_send.at[1, s], row_recv.at[1, row], row_peer(s))

    def span_forward():
        for s in range(1, SHARDS):
            peer = lax.rem(row + s, SHARDS)
            arrive(span_k.at[1, span_rows(peer), :], row_recv.at[0, peer])
            arrive(span_v.at[1, span_rows(peer), left], row_recv.at[1, peer])
        for i, (slot, to) in enumerate(((0, z_up), (2, z_down))):
            send(span_k.at[1], span_k.at[slot], span_send.at[0, i], span_recv.at[0, slot], to)
            send(span_v.at[1, :, left], span_v.at[slot, :, left], span_send.at[1, i], span_recv.at[1, slot], to)

    def neighbours_arrive():
        for slot in (0, 2):
            arrive(pre_k.at[slot], pre_recv.at[0, slot])
            arrive(pre_v.at[slot, :, left], pre_recv.at[1, slot])
            arrive(span_k.at[slot], span_recv.at[0, slot])
            arrive(span_v.at[slot, :, left], span_recv.at[1, slot])

    def project(k):
        for shard_dy in range(4):
            for f in range(2):
                a_arrive(k, f, shard_at(shard_dy, True))
        both = nn_dot(gathered[k, 0], q_mat[0:QUART, :]) + nn_dot(gathered[k, 1], q_mat[QUART:HALF, :])
        halves[k, 0] = both[:, 0:HEAD]
        halves[k, 1] = both[:, HEAD : 2 * HEAD]
        send(halves.at[k, other], halves_in.at[k], h_send.at[k], h_recv.at[k], partner)

    def finish_queries(k):
        arrive(halves_in.at[k], h_recv.at[k])
        values = halves[k, core] + halves_in[k] + qb_ref[...].astype(F32).reshape(1, HEAD)
        values = rotated(values, cos_ref[k], sin_ref[k]) * (LOG2E / math.sqrt(HEAD))
        queries[0, k] = values.astype(BF16)
        send(queries.at[0, k], queries.at[1, k], q_send.at[k, 0], q_recv.at[k, 0], device(3, 0, 0))
        send(queries.at[0, k], queries.at[2, k], q_send.at[k, 1], q_recv.at[k, 1], device(-3, 0, 0))

    key_token = lax.broadcasted_iota(jnp.int32, (1, GROUP), 1)

    def attend(k, source, first, last):
        query = queries[source, k]
        query_group = lax.rem(z + (0, 5, 3)[source], 8)
        query_token = query_group * GROUP + k * PIECE + token

        def over(slot, total, top):
            prefix = nt_dot(query, pre_k[slot]) + mask[slot]
            span = nt_dot(query, span_k[slot])
            key_group = lax.rem(z + slot + 7, 8)
            span = jnp.where(key_group * GROUP + key_token <= query_token, span, NEG)
            new_top = jnp.maximum(
                jnp.max(prefix, axis=1, keepdims=True), jnp.max(span, axis=1, keepdims=True)
            )
            if top is not None:
                new_top = jnp.maximum(new_top, top)
            blended = nn_dot(jnp.exp2(prefix - new_top).astype(BF16), pre_v[slot])
            blended = blended + nn_dot(jnp.exp2(span - new_top).astype(BF16), span_v[slot])
            if top is not None:
                blended = blended + total * jnp.exp2(top - new_top)
            return blended, new_top

        state = over(first, None, None)
        return lax.fori_loop(first + 1, last, lambda s, c: over(s, *c), state)

    def attend_own(k):
        total, top = attend(k, 0, 0, 3)
        own_o[k] = total
        own_m[k] = jnp.broadcast_to(top, (CHUNK, HEAD))

    def attend_other(k):
        for i, (source, first) in enumerate(((1, 0), (2, 1))):
            arrive(queries.at[source, k], q_recv.at[k, i])
            total, top = attend(k, source, first, 3)
            part_o[k, i] = total[:, 0:HEAD].astype(BF16)
            part_s[k, i, 0:4, :] = jnp.transpose(jnp.broadcast_to(top, (CHUNK, HEAD)))[0:4, :]
            part_s[k, i, 4:8, :] = jnp.transpose(total[:, HEAD : 2 * HEAD])[0:4, :]
            back = device(-3 if source == 1 else 3, 0, 0)
            send(part_o.at[k, i], part_o_in.at[k, i], p_send.at[k, i, 0], p_recv.at[k, i, 0], back)
            send(part_s.at[k, i], part_s_in.at[k, i], p_send.at[k, i, 1], p_recv.at[k, i, 1], back)

    def combine(k):
        total, low, top = own_o[k][:, 0:HEAD], own_o[k][:, HEAD : 2 * HEAD], own_m[k]
        for i in range(2):
            arrive(part_o_in.at[k, i], p_recv.at[k, i, 0])
            arrive(part_s_in.at[k, i], p_recv.at[k, i, 1])
            their_top = jnp.transpose(jnp.broadcast_to(part_s_in[k, i, 0:1, :], (CHUNK, HEAD)))
            their_low = jnp.transpose(jnp.broadcast_to(part_s_in[k, i, 4:5, :], (CHUNK, HEAD)))
            new_top = jnp.maximum(top, their_top)
            mine, theirs = jnp.exp2(top - new_top), jnp.exp2(their_top - new_top)
            total = total * mine + part_o_in[k, i].astype(F32) * theirs
            low = low * mine + their_low * theirs
            top = new_top
        result = (total / low).astype(BF16)
        own_head[k] = result
        attended[k, :, slot_of(head_slot(core))] = result
        for i, (cc, to) in enumerate(gatherers):
            slot = head_slot(cc)
            send(own_head.at[k], attended.at[k, :, slot_of(slot)], t_send.at[k, i], t_recv.at[k, slot], to)

    gatherers = [(0, device(0, 0, s, 0)) for s in (2, 1, 3)] + [(1, device(0, s, 0, 1)) for s in (2, 1, 3)]
    gatherers += [(other, partner)]
    gather_at, sum_at = gather_place(core), x * other + y * core

    def send_o_weight():
        for i, (cc, to) in enumerate(gatherers):
            if i < 6:
                ahead = (2, 1, 3)[i % 3]
                place = lax.rem((y if cc == 0 else x) + ahead, 4)
            else:
                place = gather_place(cc)
            for q in range(4):
                remote(
                    ow_ref.at[:, columns(cc, q, place)],
                    o_mat.at[slot_of(head_slot(cc)), pl.ds(q * 256, 256)],
                    w_send.at[1 + i], o_recv.at[head_slot(cc)], to,
                ).start()

    def other_heads(do):
        for ahead in range(1, 4):
            for c in range(2):
                do(2 * lax.rem(gather_at + ahead, 4) + c)
        do(2 * gather_at + other)

    def o_weight_arrive():
        own = o_mat.at[slot_of(head_slot(core)), :]
        pltpu.make_async_copy(own, own, local_sems.at[5]).wait()
        other_heads(lambda slot: arrive(o_mat.at[slot_of(slot), :], o_recv.at[slot]))

    def along(ahead):
        return device(0, ahead * other, ahead * core)

    def stage_one(k):
        other_heads(lambda slot: arrive(attended.at[k, :, slot_of(slot)], t_recv.at[k, slot]))
        for ahead in (2, 1, 3, 0):
            target = pl.ds(pl.multiple_of(lax.rem(sum_at + ahead, 4) * 256, 256), 256)
            value = nn_dot(attended[k], o_mat[:, target])
            if ahead == 0:
                mid[k] = value
            else:
                at = (k, ahead - 1)
                one_out[at] = value.astype(BF16)
                send(one_out.at[at], one_in.at[at], one_send.at[at], one_recv.at[at], along(ahead))

    def finish(k):
        value = mid[k]
        for i in range(3):
            arrive(one_in.at[k, i], one_recv.at[k, i])
            value = value + one_in[k, i].astype(F32)
        result = value.astype(BF16)
        for i in range(SHARDS):
            at = i * SHARD + k * PIECE
            out_ref[at : at + PIECE, :] = result[i * PIECE : (i + 1) * PIECE, :]

    a_mid(1)
    a_last(0)
    span_forward()
    a_mid(2)
    load_qw.wait()
    arrive(q_mat.at[:, pl.ds(pl.multiple_of(other * HEAD, HEAD), HEAD)], w_recv.at[0])
    project(0)
    a_last(1)
    finish_queries(0)
    a_last(2)
    send_o_weight()
    project(1)
    neighbours_arrive()
    finish_queries(1)
    attend_own(0)
    project(2)
    finish_queries(2)
    attend_other(0)
    attend_own(1)
    attend_other(1)
    attend_own(2)
    combine(0)
    attend_other(2)
    o_weight_arrive()
    stage_one(0)
    combine(1)
    stage_one(1)
    combine(2)
    finish(0)
    stage_one(2)
    finish(1)
    finish(2)

    for copy in sent:
        copy.wait_send()
    for i in range(7):
        piece = o_mat.at[slot_of(i), :]
        remote(piece, piece, w_send.at[1 + i], o_recv.at[i], partner).wait_send()


def local(
    hidden, norm_gain, q_weight, q_bias, key_weight, key_bias, value_weight, value_bias, o_weight,
    cached_key_rows, cached_value_rows, keep_blocks, kept_counts, span_start,
):
    steps = np.arange(HEAD // 2, dtype=np.float64)
    frequency = (1000000.0 ** (-2.0 * steps / HEAD)).astype(np.float32)
    frequency = np.concatenate([frequency, frequency])[None, :]

    vmem = pl.BlockSpec(memory_space=pltpu.VMEM)
    smem = pl.BlockSpec(memory_space=pltpu.SMEM)
    hbm = pl.BlockSpec(memory_space=pl.ANY)
    dma = pltpu.SemaphoreType.DMA
    scratch = [
        pltpu.VMEM((SHARD, WIDTH), BF16),
        pltpu.VMEM((CHUNKS, 2, CHUNK, QUART), BF16),
        pltpu.VMEM((HALF, 2 * HEAD), BF16),
        pltpu.VMEM((WIDTH, 2 * HEAD), BF16),
        pltpu.VMEM((8 * HEAD, 1024), BF16),
        pltpu.VMEM((32, BLOCK, HEAD), BF16),
        pltpu.VMEM((32, BLOCK, HEAD), BF16),
        pltpu.VMEM((3, KEPT, HEAD), BF16),
        pltpu.VMEM((3, KEPT, 2 * HEAD), BF16),
        pltpu.VMEM((3, GROUP, HEAD), BF16),
        pltpu.VMEM((3, GROUP, 2 * HEAD), BF16),
        pltpu.VMEM((3, 1, KEPT), F32),
        pltpu.VMEM((CHUNKS, CHUNK, HEAD), F32),
        pltpu.VMEM((CHUNKS, CHUNK, HEAD), F32),
        pltpu.VMEM((CHUNKS, 2, CHUNK, HEAD), F32),
        pltpu.VMEM((CHUNKS, CHUNK, HEAD), F32),
        pltpu.VMEM((3, CHUNKS, CHUNK, HEAD), BF16),
        pltpu.VMEM((CHUNKS, 2, CHUNK, HEAD), BF16),
        pltpu.VMEM((CHUNKS, 2, 8, CHUNK), F32),
        pltpu.VMEM((CHUNKS, 2, CHUNK, HEAD), BF16),
        pltpu.VMEM((CHUNKS, 2, 8, CHUNK), F32),
        pltpu.VMEM((CHUNKS, CHUNK, 2 * HEAD), F32),
        pltpu.VMEM((CHUNKS, CHUNK, HEAD), F32),
        pltpu.VMEM((CHUNKS, CHUNK, HEAD), BF16),
        pltpu.VMEM((CHUNKS, CHUNK, 8 * HEAD), BF16),
        pltpu.VMEM((CHUNKS, 3, CHUNK, 256), BF16),
        pltpu.VMEM((CHUNKS, 3, CHUNK, 256), BF16),
        pltpu.VMEM((CHUNKS, CHUNK, 256), F32),
        dma((6,)),
        dma((CHUNKS, 14)), dma((CHUNKS, 2, SHARDS)),
        dma((8,)), dma((1,)), dma((8,)),
        dma((2, 2)), dma((2, 3)),
        dma((2, SHARDS)), dma((2, SHARDS)),
        dma((2, 2)), dma((2, 3)),
        dma((CHUNKS,)), dma((CHUNKS,)),
        dma((CHUNKS, 2)), dma((CHUNKS, 2)),
        dma((CHUNKS, 2, 2)), dma((CHUNKS, 2, 2)),
        dma((CHUNKS, 7)), dma((CHUNKS, 8)),
        dma((CHUNKS, 3)), dma((CHUNKS, 3)),
    ]
    return pl.pallas_call(
        kernel,
        out_shape=jax.ShapeDtypeStruct((GROUP, 256), BF16),
        in_specs=[vmem, vmem, hbm, vmem, hbm, vmem, hbm, vmem, hbm, hbm, hbm, smem, smem, smem, vmem],
        out_specs=vmem,
        scratch_shapes=scratch,
        compiler_params=pltpu.CompilerParams(
            collective_id=0, has_side_effects=True, vmem_limit_bytes=56 * 1024 * 1024
        ),
        name="attention_sublayer",
    )(
        hidden, norm_gain, q_weight, q_bias, key_weight, key_bias, value_weight, value_bias, o_weight,
        cached_key_rows.reshape(32, BLOCK, HEAD), cached_value_rows.reshape(32, BLOCK, HEAD),
        keep_blocks, kept_counts, span_start, jnp.asarray(frequency),
    )


def solution(mesh):
    in_specs = (
        P(("ctx", "row"), None),
        P(),
        P(None, ("head", "row")),
        P(("head", "row")),
        P(None, "head"),
        P("head"),
        P(None, "head"),
        P("head"),
        P(("head", "row"), None),
        P("ctx", "head"),
        P("ctx", "head"),
        P("ctx", None),
        P(),
        P(),
    )
    out_specs = P("ctx", ("head", "row"))
    return jax.shard_map(local, mesh=mesh, in_specs=in_specs, out_specs=out_specs, check_vma=False)
```

```python
import math

import jax
import jax.numpy as jnp
import numpy as np
from jax import lax
from jax.experimental import pallas as pl
from jax.experimental.pallas import tpu as pltpu
from jax.sharding import PartitionSpec as P

MESH = pl.DeviceIdType.MESH
F32 = jnp.float32
BF16 = jnp.bfloat16

N_CTX = 8
WIDTH = 8192
HALF = 4096
QUART = 2048
HEAD = 128
BLOCK = 128
KEEP = 8
SHARDS = 8
SHARD = 48
CHUNKS = 3
PIECE = 16
CHUNK = SHARDS * PIECE
GROUP = SHARDS * SHARD
KEPT = KEEP * BLOCK
NEG = -1e30
LOG2E = math.log2(math.e)


def nt_dot(a, b):
    return lax.dot_general(a, b, (((1,), (1,)), ((), ())), preferred_element_type=F32)


def nn_dot(a, b):
    return lax.dot_general(a, b, (((1,), (0,)), ((), ())), preferred_element_type=F32)


def kernel(
    hidden_ref, gain_ref, qw_ref, qb_ref, kw_ref, kb_ref, vw_ref, vb_ref, ow_ref, ck_ref, cv_ref,
    blocks_ref, counts_ref, start_ref, freq_ref,
    out_ref,
    normed, gathered, q_mat, kv_mat, o_mat, cache_k, cache_v,
    pre_k, pre_v, span_k, span_v, mask, cos_ref, sin_ref,
    halves, halves_in, queries, part_o, part_s, part_o_in, part_s_in,
    own_o, own_m, own_head, attended, one_out, one_in, mid,
    local_sems, a_send, a_recv, w_send, w_recv, o_recv, pre_send, pre_recv, row_send, row_recv, span_send, span_recv,
    h_send, h_recv, q_send, q_recv, p_send, p_recv, t_send, t_recv, one_send, one_recv,
):
    z = lax.axis_index("ctx")
    head = lax.axis_index("head")
    row = lax.axis_index("row")
    core = lax.rem(head, 2)
    x_lo = row // 4
    y = lax.rem(row, 4)
    x = 2 * (head // 2) + x_lo
    other = 1 - core

    def device(dz, dx, dy, dc=None):
        xx = lax.rem(x + dx + 4, 4)
        yy = lax.rem(y + dy + 4, 4)
        cc = core if dc is None else dc
        return (lax.rem(z + dz + 8, 8), 2 * (xx // 2) + cc, 4 * lax.rem(xx, 2) + yy)

    def row_peer(step):
        return (z, head, lax.rem(row + step, SHARDS))

    partner = (z, 2 * (head // 2) + other, row)

    def remote(src, dst, send, recv, to):
        return pltpu.make_async_remote_copy(
            src_ref=src, dst_ref=dst, send_sem=send, recv_sem=recv, device_id=to, device_id_type=MESH
        )

    sent = []

    def send(src, dst, send_sem, recv_sem, to):
        copy = remote(src, dst, send_sem, recv_sem, to)
        copy.start()
        sent.append(copy)

    def arrive(dst, recv_sem):
        remote(dst, dst, recv_sem, recv_sem, partner).wait_recv()

    def load(src, dst, i):
        copy = pltpu.make_async_copy(src, dst, local_sems.at[i])
        copy.start()
        return copy

    load_k = load(ck_ref, cache_k, 0)
    load_v = load(cv_ref, cache_v, 1)
    load_kw = load(kw_ref, kv_mat.at[:, 0:HEAD], 2)
    load_vw = load(vw_ref, kv_mat.at[:, HEAD : 2 * HEAD], 3)
    own_cols = pl.ds(pl.multiple_of(core * HEAD, HEAD), HEAD)
    load_qw = load(qw_ref.at[pl.ds(pl.multiple_of(core * HALF, HALF), HALF), :], q_mat.at[:, own_cols], 4)

    def gather_place(cc):
        return y * (1 - cc) + x * cc

    def columns(cc, summed, place):
        xx = summed * (1 - cc) + place * cc
        yy = place * (1 - cc) + summed * cc
        return pl.ds(pl.multiple_of((2 * (xx // 2) + cc) * 2048 + (4 * lax.rem(xx, 2) + yy) * 256, 256), 256)

    def head_slot(cc):
        return 2 * gather_place(cc) + core

    def slot_of(index):
        return pl.ds(pl.multiple_of(index * HEAD, HEAD), HEAD)

    for q in range(4):
        pltpu.make_async_copy(
            ow_ref.at[:, columns(core, q, gather_place(core))],
            o_mat.at[slot_of(head_slot(core)), pl.ds(q * 256, 256)],
            local_sems.at[5],
        ).start()

    barrier = pltpu.get_barrier_semaphore()
    partners = [partner]
    partners += [device(0, s, 0, c) for s in range(1, 4) for c in range(2)]
    partners += [device(0, 0, s, c) for s in range(1, 4) for c in range(2)]
    beside = 4 * (1 - x_lo)
    partners += [(z, head, beside + lax.rem(y + s, 4)) for s in range(1, 4)]
    partners += [device(dz, 0, 0) for dz in (1, -1, 3, -3)]
    for to in partners:
        pl.semaphore_signal(barrier, inc=1, device_id=to, device_id_type=MESH)

    def rows_of(shard):
        return pl.ds(pl.multiple_of(shard * PIECE, PIECE), PIECE)

    def normalise(k):
        rows = slice(k * PIECE, (k + 1) * PIECE)
        total = jnp.zeros((PIECE, 1), F32)
        for i in range(8):
            part = hidden_ref[rows, i * 1024 : (i + 1) * 1024].astype(F32)
            total = total + jnp.sum(part * part, axis=1, keepdims=True)
        factor = lax.rsqrt(total / WIDTH + 1e-6)
        for i in range(8):
            cols = slice(i * 1024, (i + 1) * 1024)
            part = hidden_ref[rows, cols].astype(F32) * factor * gain_ref[cols].astype(F32).reshape(1, 1024)
            normed[rows, cols] = part.astype(BF16)
        for f in range(2):
            cols = pl.ds(pl.multiple_of(core * HALF + f * QUART, QUART), QUART)
            gathered[k, f, rows_of(row), :] = normed[rows, cols]

    y_up, y_down = device(0, 0, 1), device(0, 0, -1)
    x_up, x_down = device(0, 1, 0), device(0, -1, 0)
    a_count = [0, 0, 0]

    def forward(k, f, shard, to):
        piece = gathered.at[k, f, rows_of(shard), :]
        send(piece, piece, a_send.at[k, a_count[k]], a_recv.at[k, f, shard], to)
        a_count[k] += 1

    def shard_at(dy, flip=False):
        xl = 1 - x_lo if flip else x_lo
        return 4 * xl + lax.rem(y + dy + 4, 4)

    def a_arrive(k, f, shard):
        arrive(gathered.at[k, f, rows_of(shard), :], a_recv.at[k, f, shard])

    def a_start(k):
        forward(k, 0, row, x_up)
        forward(k, 0, row, y_up)
        forward(k, 1, row, x_down)
        forward(k, 1, row, y_down)
        forward(k, 1, row, y_up)
        forward(k, 0, row, y_down)

    def a_mid(k):
        below, above = shard_at(-1), shard_at(1)
        a_arrive(k, 0, below)
        forward(k, 0, below, y_up)
        forward(k, 0, below, x_up)
        a_arrive(k, 1, above)
        forward(k, 1, above, y_down)
        forward(k, 1, above, x_down)
        a_arrive(k, 1, below)
        forward(k, 1, below, x_down)
        a_arrive(k, 0, above)
        forward(k, 0, above, x_up)

    def a_last(k):
        far = shard_at(2)
        a_arrive(k, 0, far)
        forward(k, 0, far, x_up)
        a_arrive(k, 1, far)
        forward(k, 1, far, x_down)

    normalise(0)
    normalise(1)
    normalise(2)
    pl.semaphore_wait(barrier, len(partners))
    a_start(0)
    a_start(1)

    send(
        qw_ref.at[pl.ds(pl.multiple_of(other * HALF, HALF), HALF), :],
        q_mat.at[:, own_cols], w_send.at[0], w_recv.at[0], partner,
    )
    load_k.wait()
    load_v.wait()
    for j in range(KEEP):
        pre_k[1, j * BLOCK : (j + 1) * BLOCK, :] = cache_k[blocks_ref[0, j]]
        pre_v[1, j * BLOCK : (j + 1) * BLOCK, 0:HEAD] = cache_v[blocks_ref[0, j]]
    z_up, z_down = device(1, 0, 0), device(-1, 0, 0)
    left = pl.ds(0, HEAD)
    for s in range(3):
        pre_v[s, :, HEAD : 2 * HEAD] = jnp.ones((KEPT, HEAD), BF16)
        span_v[s, :, HEAD : 2 * HEAD] = jnp.ones((GROUP, HEAD), BF16)
        live = counts_ref[lax.rem(z + s + 7, N_CTX)]
        slot_index = lax.broadcasted_iota(jnp.int32, (1, KEPT), 1) // BLOCK
        mask[s] = jnp.where(slot_index < live, 0.0, NEG).astype(F32)

    token = lax.broadcasted_iota(jnp.int32, (CHUNK, 1), 0)
    token = (token // PIECE) * SHARD + lax.rem(token, PIECE)
    sign = jnp.where(lax.broadcasted_iota(jnp.int32, (1, HEAD), 1) < HEAD // 2, -1.0, 1.0)

    def angles_of(k):
        positions = (start_ref[0] + z * GROUP + k * PIECE + token).astype(F32)
        angles = positions * freq_ref[...]
        cos_ref[k] = jnp.cos(angles)
        sin_ref[k] = jnp.sin(angles) * sign

    for k in range(CHUNKS):
        angles_of(k)

    def rotated(values, cosine, sine):
        return values * cosine + pltpu.roll(values, HEAD // 2, 1) * sine

    load_kw.wait()
    load_vw.wait()

    def kv_step(i, total):
        at = pl.ds(pl.multiple_of(i * 1024, 1024), 1024)
        return total + nn_dot(normed[:, at], kv_mat[at, :])

    def span_rows(shard):
        return pl.ds(pl.multiple_of(shard * SHARD, SHARD), SHARD)

    pair = lax.fori_loop(0, 4, kv_step, jnp.zeros((SHARD, 2 * HEAD), F32))
    a_mid(0)
    a_start(2)
    for i, (slot, to) in enumerate(((0, z_up), (2, z_down))):
        send(pre_k.at[1], pre_k.at[slot], pre_send.at[0, i], pre_recv.at[0, slot], to)
        send(pre_v.at[1, :, left], pre_v.at[slot, :, left], pre_send.at[1, i], pre_recv.at[1, slot], to)

    pair = lax.fori_loop(4, 8, kv_step, pair)
    key_part = pair[:, 0:HEAD] + kb_ref[...].astype(F32).reshape(1, HEAD)
    value_part = pair[:, HEAD : 2 * HEAD] + vb_ref[...].astype(F32).reshape(1, HEAD)
    own_cos = jnp.concatenate([cos_ref[k, rows_of(row), :] for k in range(CHUNKS)], axis=0)
    own_sin = jnp.concatenate([sin_ref[k, rows_of(row), :] for k in range(CHUNKS)], axis=0)

    span_k[1, span_rows(row), :] = rotated(key_part, own_cos, own_sin).astype(BF16)
    span_v[1, span_rows(row), 0:HEAD] = value_part.astype(BF16)
    for s in range(1, SHARDS):
        here = span_k.at[1, span_rows(row), :]
        send(here, here, row_send.at[0, s], row_recv.at[0, row], row_peer(s))
        here = span_v.at[1, span_rows(row), left]
        send(here, here, row_send.at[1, s], row_recv.at[1, row], row_peer(s))

    def span_forward():
        for s in range(1, SHARDS):
            peer = lax.rem(row + s, SHARDS)
            arrive(span_k.at[1, span_rows(peer), :], row_recv.at[0, peer])
            arrive(span_v.at[1, span_rows(peer), left], row_recv.at[1, peer])
        for i, (slot, to) in enumerate(((0, z_up), (2, z_down))):
            send(span_k.at[1], span_k.at[slot], span_send.at[0, i], span_recv.at[0, slot], to)
            send(span_v.at[1, :, left], span_v.at[slot, :, left], span_send.at[1, i], span_recv.at[1, slot], to)

    def neighbours_arrive():
        for slot in (0, 2):
            arrive(pre_k.at[slot], pre_recv.at[0, slot])
            arrive(pre_v.at[slot, :, left], pre_recv.at[1, slot])
            arrive(span_k.at[slot], span_recv.at[0, slot])
            arrive(span_v.at[slot, :, left], span_recv.at[1, slot])

    def project(k):
        for shard_dy in range(4):
            for f in range(2):
                a_arrive(k, f, shard_at(shard_dy, True))
        both = nn_dot(gathered[k, 0], q_mat[0:QUART, :]) + nn_dot(gathered[k, 1], q_mat[QUART:HALF, :])
        halves[k, 0] = both[:, 0:HEAD]
        halves[k, 1] = both[:, HEAD : 2 * HEAD]
        send(halves.at[k, other], halves_in.at[k], h_send.at[k], h_recv.at[k], partner)

    def finish_queries(k):
        arrive(halves_in.at[k], h_recv.at[k])
        values = halves[k, core] + halves_in[k] + qb_ref[...].astype(F32).reshape(1, HEAD)
        values = rotated(values, cos_ref[k], sin_ref[k]) * (LOG2E / math.sqrt(HEAD))
        queries[0, k] = values.astype(BF16)
        send(queries.at[0, k], queries.at[1, k], q_send.at[k, 0], q_recv.at[k, 0], device(3, 0, 0))
        send(queries.at[0, k], queries.at[2, k], q_send.at[k, 1], q_recv.at[k, 1], device(-3, 0, 0))

    key_token = lax.broadcasted_iota(jnp.int32, (1, GROUP), 1)

    def tokens_of(source, chunks):
        group = lax.rem(z + (0, 5, 3)[source], N_CTX)
        return jnp.concatenate([group * GROUP + k * PIECE + token for k in chunks], axis=0)

    def over(query, query_token, slot, total, top):
        prefix = nt_dot(query, pre_k[slot]) + mask[slot]
        span = nt_dot(query, span_k[slot])
        key_group = lax.rem(z + slot + 7, N_CTX)
        span = jnp.where(key_group * GROUP + key_token <= query_token, span, NEG)
        new_top = jnp.maximum(jnp.max(prefix, axis=1, keepdims=True), jnp.max(span, axis=1, keepdims=True))
        if top is not None:
            new_top = jnp.maximum(new_top, top)
        blended = nn_dot(jnp.exp2(prefix - new_top).astype(BF16), pre_v[slot])
        blended = blended + nn_dot(jnp.exp2(span - new_top).astype(BF16), span_v[slot])
        if top is not None:
            blended = blended + total * jnp.exp2(top - new_top)
        return blended, new_top

    def attend(query, query_token, first):
        state = over(query, query_token, first, None, None)
        return lax.fori_loop(first + 1, 3, lambda s, c: over(query, query_token, s, *c), state)

    def attend_own():
        total, top = attend(queries[0].reshape(GROUP, HEAD), tokens_of(0, range(CHUNKS)), 0)
        for k in range(CHUNKS):
            rows = slice(k * CHUNK, (k + 1) * CHUNK)
            own_o[k] = total[rows]
            own_m[k] = jnp.broadcast_to(top[rows], (CHUNK, HEAD))

    def give_back(k, i, total, top):
        part_o[k, i] = total[:, 0:HEAD].astype(BF16)
        part_s[k, i, 0:4, :] = jnp.transpose(jnp.broadcast_to(top, (CHUNK, HEAD)))[0:4, :]
        part_s[k, i, 4:8, :] = jnp.transpose(total[:, HEAD : 2 * HEAD])[0:4, :]
        back = device((-3, 3)[i], 0, 0)
        send(part_o.at[k, i], part_o_in.at[k, i], p_send.at[k, i, 0], p_recv.at[k, i, 0], back)
        send(part_s.at[k, i], part_s_in.at[k, i], p_send.at[k, i, 1], p_recv.at[k, i, 1], back)

    def attend_early():
        for i, (source, first) in enumerate(((1, 0), (2, 1))):
            for k in range(2):
                arrive(queries.at[source, k], q_recv.at[k, i])
            query = queries[source, 0:2].reshape(2 * CHUNK, HEAD)
            total, top = attend(query, tokens_of(source, range(2)), first)
            for k in range(2):
                rows = slice(k * CHUNK, (k + 1) * CHUNK)
                give_back(k, i, total[rows], top[rows])

    def attend_last():
        arrive(queries.at[1, 2], q_recv.at[2, 0])
        arrive(queries.at[2, 2], q_recv.at[2, 1])
        below, above = tokens_of(1, (2,)), tokens_of(2, (2,))
        total, top = over(queries[1, 2], below, 0, None, None)
        query = jnp.concatenate([queries[1, 2], queries[2, 2]], axis=0)
        query_token = jnp.concatenate([below, above], axis=0)
        state = (
            jnp.concatenate([total, jnp.zeros((CHUNK, 2 * HEAD), F32)], axis=0),
            jnp.concatenate([top, jnp.full((CHUNK, 1), NEG, F32)], axis=0),
        )
        total, top = lax.fori_loop(1, 3, lambda s, c: over(query, query_token, s, *c), state)
        give_back(2, 0, total[0:CHUNK], top[0:CHUNK])
        give_back(2, 1, total[CHUNK : 2 * CHUNK], top[CHUNK : 2 * CHUNK])

    def combine(k):
        total, low, top = own_o[k][:, 0:HEAD], own_o[k][:, HEAD : 2 * HEAD], own_m[k]
        for i in range(2):
            arrive(part_o_in.at[k, i], p_recv.at[k, i, 0])
            arrive(part_s_in.at[k, i], p_recv.at[k, i, 1])
            their_top = jnp.transpose(jnp.broadcast_to(part_s_in[k, i, 0:1, :], (CHUNK, HEAD)))
            their_low = jnp.transpose(jnp.broadcast_to(part_s_in[k, i, 4:5, :], (CHUNK, HEAD)))
            new_top = jnp.maximum(top, their_top)
            mine, theirs = jnp.exp2(top - new_top), jnp.exp2(their_top - new_top)
            total = total * mine + part_o_in[k, i].astype(F32) * theirs
            low = low * mine + their_low * theirs
            top = new_top
        result = (total / low).astype(BF16)
        own_head[k] = result
        attended[k, :, slot_of(head_slot(core))] = result
        for i, (cc, to) in enumerate(gatherers):
            slot = head_slot(cc)
            send(own_head.at[k], attended.at[k, :, slot_of(slot)], t_send.at[k, i], t_recv.at[k, slot], to)

    gatherers = [(0, device(0, 0, s, 0)) for s in (2, 1, 3)] + [(1, device(0, s, 0, 1)) for s in (2, 1, 3)]
    gatherers += [(other, partner)]
    gather_at, sum_at = gather_place(core), x * other + y * core

    def send_o_weight():
        for i, (cc, to) in enumerate(gatherers):
            if i < 6:
                ahead = (2, 1, 3)[i % 3]
                place = lax.rem((y if cc == 0 else x) + ahead, 4)
            else:
                place = gather_place(cc)
            for q in range(4):
                remote(
                    ow_ref.at[:, columns(cc, q, place)],
                    o_mat.at[slot_of(head_slot(cc)), pl.ds(q * 256, 256)],
                    w_send.at[1 + i], o_recv.at[head_slot(cc)], to,
                ).start()

    def other_heads(do):
        for ahead in range(1, 4):
            for c in range(2):
                do(2 * lax.rem(gather_at + ahead, 4) + c)
        do(2 * gather_at + other)

    def o_weight_arrive():
        own = o_mat.at[slot_of(head_slot(core)), :]
        pltpu.make_async_copy(own, own, local_sems.at[5]).wait()
        other_heads(lambda slot: arrive(o_mat.at[slot_of(slot), :], o_recv.at[slot]))

    def along(ahead):
        return device(0, ahead * other, ahead * core)

    def stage_one(k):
        other_heads(lambda slot: arrive(attended.at[k, :, slot_of(slot)], t_recv.at[k, slot]))
        for ahead in (2, 1, 3, 0):
            target = pl.ds(pl.multiple_of(lax.rem(sum_at + ahead, 4) * 256, 256), 256)
            value = nn_dot(attended[k], o_mat[:, target])
            if ahead == 0:
                mid[k] = value
            else:
                at = (k, ahead - 1)
                one_out[at] = value.astype(BF16)
                send(one_out.at[at], one_in.at[at], one_send.at[at], one_recv.at[at], along(ahead))

    def finish(k):
        value = mid[k]
        for i in range(3):
            arrive(one_in.at[k, i], one_recv.at[k, i])
            value = value + one_in[k, i].astype(F32)
        result = value.astype(BF16)
        for i in range(SHARDS):
            at = i * SHARD + k * PIECE
            out_ref[at : at + PIECE, :] = result[i * PIECE : (i + 1) * PIECE, :]

    a_mid(1)
    a_last(0)
    span_forward()
    a_mid(2)
    load_qw.wait()
    arrive(q_mat.at[:, pl.ds(pl.multiple_of(other * HEAD, HEAD), HEAD)], w_recv.at[0])
    project(0)
    a_last(1)
    finish_queries(0)
    a_last(2)
    project(1)
    finish_queries(1)
    project(2)
    finish_queries(2)
    send_o_weight()
    neighbours_arrive()
    attend_own()
    attend_early()
    attend_last()
    combine(0)
    combine(1)
    o_weight_arrive()
    stage_one(0)
    combine(2)
    stage_one(1)
    stage_one(2)
    finish(0)
    finish(1)
    finish(2)

    for copy in sent:
        copy.wait_send()
    for i in range(7):
        piece = o_mat.at[slot_of(i), :]
        remote(piece, piece, w_send.at[1 + i], o_recv.at[i], partner).wait_send()


def local(
    hidden, norm_gain, q_weight, q_bias, key_weight, key_bias, value_weight, value_bias, o_weight,
    cached_key_rows, cached_value_rows, keep_blocks, kept_counts, span_start,
):
    steps = np.arange(HEAD // 2, dtype=np.float64)
    frequency = (1000000.0 ** (-2.0 * steps / HEAD)).astype(np.float32)
    frequency = np.concatenate([frequency, frequency])[None, :]

    vmem = pl.BlockSpec(memory_space=pltpu.VMEM)
    smem = pl.BlockSpec(memory_space=pltpu.SMEM)
    hbm = pl.BlockSpec(memory_space=pl.ANY)
    dma = pltpu.SemaphoreType.DMA
    scratch = [
        pltpu.VMEM((SHARD, WIDTH), BF16),
        pltpu.VMEM((CHUNKS, 2, CHUNK, QUART), BF16),
        pltpu.VMEM((HALF, 2 * HEAD), BF16),
        pltpu.VMEM((WIDTH, 2 * HEAD), BF16),
        pltpu.VMEM((8 * HEAD, 1024), BF16),
        pltpu.VMEM((32, BLOCK, HEAD), BF16),
        pltpu.VMEM((32, BLOCK, HEAD), BF16),
        pltpu.VMEM((3, KEPT, HEAD), BF16),
        pltpu.VMEM((3, KEPT, 2 * HEAD), BF16),
        pltpu.VMEM((3, GROUP, HEAD), BF16),
        pltpu.VMEM((3, GROUP, 2 * HEAD), BF16),
        pltpu.VMEM((3, 1, KEPT), F32),
        pltpu.VMEM((CHUNKS, CHUNK, HEAD), F32),
        pltpu.VMEM((CHUNKS, CHUNK, HEAD), F32),
        pltpu.VMEM((CHUNKS, 2, CHUNK, HEAD), F32),
        pltpu.VMEM((CHUNKS, CHUNK, HEAD), F32),
        pltpu.VMEM((3, CHUNKS, CHUNK, HEAD), BF16),
        pltpu.VMEM((CHUNKS, 2, CHUNK, HEAD), BF16),
        pltpu.VMEM((CHUNKS, 2, 8, CHUNK), F32),
        pltpu.VMEM((CHUNKS, 2, CHUNK, HEAD), BF16),
        pltpu.VMEM((CHUNKS, 2, 8, CHUNK), F32),
        pltpu.VMEM((CHUNKS, CHUNK, 2 * HEAD), F32),
        pltpu.VMEM((CHUNKS, CHUNK, HEAD), F32),
        pltpu.VMEM((CHUNKS, CHUNK, HEAD), BF16),
        pltpu.VMEM((CHUNKS, CHUNK, 8 * HEAD), BF16),
        pltpu.VMEM((CHUNKS, 3, CHUNK, 256), BF16),
        pltpu.VMEM((CHUNKS, 3, CHUNK, 256), BF16),
        pltpu.VMEM((CHUNKS, CHUNK, 256), F32),
        dma((6,)),
        dma((CHUNKS, 14)), dma((CHUNKS, 2, SHARDS)),
        dma((8,)), dma((1,)), dma((8,)),
        dma((2, 2)), dma((2, 3)),
        dma((2, SHARDS)), dma((2, SHARDS)),
        dma((2, 2)), dma((2, 3)),
        dma((CHUNKS,)), dma((CHUNKS,)),
        dma((CHUNKS, 2)), dma((CHUNKS, 2)),
        dma((CHUNKS, 2, 2)), dma((CHUNKS, 2, 2)),
        dma((CHUNKS, 7)), dma((CHUNKS, 8)),
        dma((CHUNKS, 3)), dma((CHUNKS, 3)),
    ]
    return pl.pallas_call(
        kernel,
        out_shape=jax.ShapeDtypeStruct((GROUP, 256), BF16),
        in_specs=[vmem, vmem, hbm, vmem, hbm, vmem, hbm, vmem, hbm, hbm, hbm, smem, smem, smem, vmem],
        out_specs=vmem,
        scratch_shapes=scratch,
        compiler_params=pltpu.CompilerParams(
            collective_id=0, has_side_effects=True, vmem_limit_bytes=56 * 1024 * 1024
        ),
        name="attention_sublayer",
    )(
        hidden, norm_gain, q_weight, q_bias, key_weight, key_bias, value_weight, value_bias, o_weight,
        cached_key_rows.reshape(32, BLOCK, HEAD), cached_value_rows.reshape(32, BLOCK, HEAD),
        keep_blocks, kept_counts, span_start, jnp.asarray(frequency),
    )


def solution(mesh):
    in_specs = (
        P(("ctx", "row"), None),
        P(),
        P(None, ("head", "row")),
        P(("head", "row")),
        P(None, "head"),
        P("head"),
        P(None, "head"),
        P("head"),
        P(("head", "row"), None),
        P("ctx", "head"),
        P("ctx", "head"),
        P("ctx", None),
        P(),
        P(),
    )
    out_specs = P("ctx", ("head", "row"))
    return jax.shard_map(local, mesh=mesh, in_specs=in_specs, out_specs=out_specs, check_vma=False)
```

```python
import math

import jax
import jax.numpy as jnp
import numpy as np
from jax import lax
from jax.experimental import pallas as pl
from jax.experimental.pallas import tpu as pltpu
from jax.sharding import PartitionSpec as P

MESH = pl.DeviceIdType.MESH
F32 = jnp.float32
BF16 = jnp.bfloat16

N_CTX = 8
WIDTH = 8192
HALF = 4096
QUART = 2048
HEAD = 128
BLOCK = 128
KEEP = 8
SHARDS = 8
SHARD = 48
CHUNKS = 3
PIECE = 16
CHUNK = SHARDS * PIECE
GROUP = SHARDS * SHARD
KEPT = KEEP * BLOCK
NEG = -1e30
LOG2E = math.log2(math.e)


def nt_dot(a, b):
    return lax.dot_general(a, b, (((1,), (1,)), ((), ())), preferred_element_type=F32)


def nn_dot(a, b):
    return lax.dot_general(a, b, (((1,), (0,)), ((), ())), preferred_element_type=F32)


def kernel(
    hidden_hbm, gain_ref, qw_ref, qb_ref, kw_ref, kb_ref, vw_ref, vb_ref, ow_ref, ck_ref, cv_ref,
    blocks_ref, counts_ref, start_ref, freq_ref,
    out_ref,
    hidden_ref, normed, gathered, q_mat, kv_mat, o_mat, cache_k, cache_v,
    pre_k, pre_v, span_k, span_v, mask, cos_ref, sin_ref,
    halves, halves_in, queries, part_o, part_s, part_o_in, part_s_in,
    own_o, own_m, own_head, attended, one_out, one_in, mid,
    local_sems, a_send, a_recv, w_send, w_recv, o_recv, pre_send, pre_recv, row_send, row_recv, span_send, span_recv,
    h_send, h_recv, q_send, q_recv, p_send, p_recv, t_send, t_recv, one_send, one_recv,
):
    z = lax.axis_index("ctx")
    head = lax.axis_index("head")
    row = lax.axis_index("row")
    core = lax.rem(head, 2)
    x_lo = row // 4
    y = lax.rem(row, 4)
    x = 2 * (head // 2) + x_lo
    other = 1 - core

    def device(dz, dx, dy, dc=None):
        xx = lax.rem(x + dx + 4, 4)
        yy = lax.rem(y + dy + 4, 4)
        cc = core if dc is None else dc
        return (lax.rem(z + dz + 8, 8), 2 * (xx // 2) + cc, 4 * lax.rem(xx, 2) + yy)

    def row_peer(step):
        return (z, head, lax.rem(row + step, SHARDS))

    partner = (z, 2 * (head // 2) + other, row)

    def remote(src, dst, send, recv, to):
        return pltpu.make_async_remote_copy(
            src_ref=src, dst_ref=dst, send_sem=send, recv_sem=recv, device_id=to, device_id_type=MESH
        )

    barrier = pltpu.get_barrier_semaphore()
    partners = [partner]
    partners += [device(0, s, 0, c) for s in range(1, 4) for c in range(2)]
    partners += [device(0, 0, s, c) for s in range(1, 4) for c in range(2)]
    beside = 4 * (1 - x_lo)
    partners += [(z, head, beside + lax.rem(y + s, 4)) for s in range(1, 4)]
    partners += [device(dz, 0, 0) for dz in (1, -1, 3, -3)]
    for to in partners:
        pl.semaphore_signal(barrier, inc=1, device_id=to, device_id_type=MESH)

    sent = []

    def send(src, dst, send_sem, recv_sem, to):
        copy = remote(src, dst, send_sem, recv_sem, to)
        copy.start()
        sent.append(copy)

    def arrive(dst, recv_sem):
        remote(dst, dst, recv_sem, recv_sem, partner).wait_recv()

    def load(src, dst, i):
        copy = pltpu.make_async_copy(src, dst, local_sems.at[i])
        copy.start()
        return copy

    load_hidden = load(hidden_hbm, hidden_ref, 6)
    load_k = load(ck_ref, cache_k, 0)
    load_v = load(cv_ref, cache_v, 1)
    load_kw = load(kw_ref, kv_mat.at[:, 0:HEAD], 2)
    load_vw = load(vw_ref, kv_mat.at[:, HEAD : 2 * HEAD], 3)
    own_cols = pl.ds(pl.multiple_of(core * HEAD, HEAD), HEAD)
    load_qw = load(qw_ref.at[pl.ds(pl.multiple_of(core * HALF, HALF), HALF), :], q_mat.at[:, own_cols], 4)

    def gather_place(cc):
        return y * (1 - cc) + x * cc

    def columns(cc, summed, place):
        xx = summed * (1 - cc) + place * cc
        yy = place * (1 - cc) + summed * cc
        return pl.ds(pl.multiple_of((2 * (xx // 2) + cc) * 2048 + (4 * lax.rem(xx, 2) + yy) * 256, 256), 256)

    def head_slot(cc):
        return 2 * gather_place(cc) + core

    def slot_of(index):
        return pl.ds(pl.multiple_of(index * HEAD, HEAD), HEAD)

    for q in range(4):
        pltpu.make_async_copy(
            ow_ref.at[:, columns(core, q, gather_place(core))],
            o_mat.at[slot_of(head_slot(core)), pl.ds(q * 256, 256)],
            local_sems.at[5],
        ).start()

    def rows_of(shard):
        return pl.ds(pl.multiple_of(shard * PIECE, PIECE), PIECE)

    def normalise(k):
        rows = slice(k * PIECE, (k + 1) * PIECE)
        total = jnp.zeros((PIECE, 1), F32)
        for i in range(8):
            part = hidden_ref[rows, i * 1024 : (i + 1) * 1024].astype(F32)
            total = total + jnp.sum(part * part, axis=1, keepdims=True)
        factor = lax.rsqrt(total / WIDTH + 1e-6)
        for i in range(8):
            cols = slice(i * 1024, (i + 1) * 1024)
            part = hidden_ref[rows, cols].astype(F32) * factor * gain_ref[cols].astype(F32).reshape(1, 1024)
            normed[rows, cols] = part.astype(BF16)
        for f in range(2):
            cols = pl.ds(pl.multiple_of(core * HALF + f * QUART, QUART), QUART)
            gathered[k, f, rows_of(row), :] = normed[rows, cols]

    y_up, y_down = device(0, 0, 1), device(0, 0, -1)
    x_up, x_down = device(0, 1, 0), device(0, -1, 0)
    a_count = [0, 0, 0]

    def forward(k, f, shard, to):
        piece = gathered.at[k, f, rows_of(shard), :]
        send(piece, piece, a_send.at[k, a_count[k]], a_recv.at[k, f, shard], to)
        a_count[k] += 1

    def shard_at(dy, flip=False):
        xl = 1 - x_lo if flip else x_lo
        return 4 * xl + lax.rem(y + dy + 4, 4)

    def a_arrive(k, f, shard):
        arrive(gathered.at[k, f, rows_of(shard), :], a_recv.at[k, f, shard])

    def a_start(k):
        forward(k, 0, row, x_up)
        forward(k, 0, row, y_up)
        forward(k, 1, row, x_down)
        forward(k, 1, row, y_down)
        forward(k, 1, row, y_up)
        forward(k, 0, row, y_down)

    def a_mid(k):
        below, above = shard_at(-1), shard_at(1)
        a_arrive(k, 0, below)
        forward(k, 0, below, y_up)
        forward(k, 0, below, x_up)
        a_arrive(k, 1, above)
        forward(k, 1, above, y_down)
        forward(k, 1, above, x_down)
        a_arrive(k, 1, below)
        forward(k, 1, below, x_down)
        a_arrive(k, 0, above)
        forward(k, 0, above, x_up)

    def a_last(k):
        far = shard_at(2)
        a_arrive(k, 0, far)
        forward(k, 0, far, x_up)
        a_arrive(k, 1, far)
        forward(k, 1, far, x_down)

    load_hidden.wait()
    normalise(0)
    normalise(1)
    normalise(2)
    pl.semaphore_wait(barrier, len(partners))
    a_start(0)
    a_start(1)

    send(
        qw_ref.at[pl.ds(pl.multiple_of(other * HALF, HALF), HALF), :],
        q_mat.at[:, own_cols], w_send.at[0], w_recv.at[0], partner,
    )
    load_k.wait()
    load_v.wait()
    for j in range(KEEP):
        pre_k[1, j * BLOCK : (j + 1) * BLOCK, :] = cache_k[blocks_ref[0, j]]
        pre_v[1, j * BLOCK : (j + 1) * BLOCK, 0:HEAD] = cache_v[blocks_ref[0, j]]
    z_up, z_down = device(1, 0, 0), device(-1, 0, 0)
    left = pl.ds(0, HEAD)
    for s in range(3):
        pre_v[s, :, HEAD : 2 * HEAD] = jnp.ones((KEPT, HEAD), BF16)
        span_v[s, :, HEAD : 2 * HEAD] = jnp.ones((GROUP, HEAD), BF16)
        live = counts_ref[lax.rem(z + s + 7, N_CTX)]
        slot_index = lax.broadcasted_iota(jnp.int32, (1, KEPT), 1) // BLOCK
        mask[s] = jnp.where(slot_index < live, 0.0, NEG).astype(F32)

    token = lax.broadcasted_iota(jnp.int32, (CHUNK, 1), 0)
    token = (token // PIECE) * SHARD + lax.rem(token, PIECE)
    sign = jnp.where(lax.broadcasted_iota(jnp.int32, (1, HEAD), 1) < HEAD // 2, -1.0, 1.0)

    def angles_of(k):
        positions = (start_ref[0] + z * GROUP + k * PIECE + token).astype(F32)
        angles = positions * freq_ref[...]
        cos_ref[k] = jnp.cos(angles)
        sin_ref[k] = jnp.sin(angles) * sign

    for k in range(CHUNKS):
        angles_of(k)

    def rotated(values, cosine, sine):
        return values * cosine + pltpu.roll(values, HEAD // 2, 1) * sine

    load_kw.wait()
    load_vw.wait()

    def kv_step(i, total):
        at = pl.ds(pl.multiple_of(i * 1024, 1024), 1024)
        return total + nn_dot(normed[:, at], kv_mat[at, :])

    def span_rows(shard):
        return pl.ds(pl.multiple_of(shard * SHARD, SHARD), SHARD)

    pair = lax.fori_loop(0, 4, kv_step, jnp.zeros((SHARD, 2 * HEAD), F32))
    a_mid(0)
    a_start(2)
    for i, (slot, to) in enumerate(((0, z_up), (2, z_down))):
        send(pre_k.at[1], pre_k.at[slot], pre_send.at[0, i], pre_recv.at[0, slot], to)
        send(pre_v.at[1, :, left], pre_v.at[slot, :, left], pre_send.at[1, i], pre_recv.at[1, slot], to)

    pair = lax.fori_loop(4, 8, kv_step, pair)
    key_part = pair[:, 0:HEAD] + kb_ref[...].astype(F32).reshape(1, HEAD)
    value_part = pair[:, HEAD : 2 * HEAD] + vb_ref[...].astype(F32).reshape(1, HEAD)
    own_cos = jnp.concatenate([cos_ref[k, rows_of(row), :] for k in range(CHUNKS)], axis=0)
    own_sin = jnp.concatenate([sin_ref[k, rows_of(row), :] for k in range(CHUNKS)], axis=0)

    span_k[1, span_rows(row), :] = rotated(key_part, own_cos, own_sin).astype(BF16)
    span_v[1, span_rows(row), 0:HEAD] = value_part.astype(BF16)
    for s in range(1, SHARDS):
        here = span_k.at[1, span_rows(row), :]
        send(here, here, row_send.at[0, s], row_recv.at[0, row], row_peer(s))
        here = span_v.at[1, span_rows(row), left]
        send(here, here, row_send.at[1, s], row_recv.at[1, row], row_peer(s))

    def span_forward():
        for s in range(1, SHARDS):
            peer = lax.rem(row + s, SHARDS)
            arrive(span_k.at[1, span_rows(peer), :], row_recv.at[0, peer])
            arrive(span_v.at[1, span_rows(peer), left], row_recv.at[1, peer])
        for i, (slot, to) in enumerate(((0, z_up), (2, z_down))):
            send(span_k.at[1], span_k.at[slot], span_send.at[0, i], span_recv.at[0, slot], to)
            send(span_v.at[1, :, left], span_v.at[slot, :, left], span_send.at[1, i], span_recv.at[1, slot], to)

    def neighbours_arrive():
        for slot in (0, 2):
            arrive(pre_k.at[slot], pre_recv.at[0, slot])
            arrive(pre_v.at[slot, :, left], pre_recv.at[1, slot])
            arrive(span_k.at[slot], span_recv.at[0, slot])
            arrive(span_v.at[slot, :, left], span_recv.at[1, slot])

    def project(k):
        for shard_dy in range(4):
            for f in range(2):
                a_arrive(k, f, shard_at(shard_dy, True))
        both = nn_dot(gathered[k, 0], q_mat[0:QUART, :]) + nn_dot(gathered[k, 1], q_mat[QUART:HALF, :])
        halves[k, 0] = both[:, 0:HEAD]
        halves[k, 1] = both[:, HEAD : 2 * HEAD]
        send(halves.at[k, other], halves_in.at[k], h_send.at[k], h_recv.at[k], partner)

    def finish_queries(k):
        arrive(halves_in.at[k], h_recv.at[k])
        values = halves[k, core] + halves_in[k] + qb_ref[...].astype(F32).reshape(1, HEAD)
        values = rotated(values, cos_ref[k], sin_ref[k]) * (LOG2E / math.sqrt(HEAD))
        queries[0, k] = values.astype(BF16)
        send(queries.at[0, k], queries.at[1, k], q_send.at[k, 0], q_recv.at[k, 0], device(3, 0, 0))
        send(queries.at[0, k], queries.at[2, k], q_send.at[k, 1], q_recv.at[k, 1], device(-3, 0, 0))

    key_token = lax.broadcasted_iota(jnp.int32, (1, GROUP), 1)

    def tokens_of(source, chunks):
        group = lax.rem(z + (0, 5, 3)[source], N_CTX)
        return jnp.concatenate([group * GROUP + k * PIECE + token for k in chunks], axis=0)

    def over(query, query_token, slot, total, top):
        prefix = nt_dot(query, pre_k[slot]) + mask[slot]
        span = nt_dot(query, span_k[slot])
        key_group = lax.rem(z + slot + 7, N_CTX)
        span = jnp.where(key_group * GROUP + key_token <= query_token, span, NEG)
        new_top = jnp.maximum(jnp.max(prefix, axis=1, keepdims=True), jnp.max(span, axis=1, keepdims=True))
        if top is not None:
            new_top = jnp.maximum(new_top, top)
        blended = nn_dot(jnp.exp2(prefix - new_top).astype(BF16), pre_v[slot])
        blended = blended + nn_dot(jnp.exp2(span - new_top).astype(BF16), span_v[slot])
        if top is not None:
            blended = blended + total * jnp.exp2(top - new_top)
        return blended, new_top

    def attend(query, query_token, first):
        state = over(query, query_token, first, None, None)
        return lax.fori_loop(first + 1, 3, lambda s, c: over(query, query_token, s, *c), state)

    def attend_own():
        total, top = attend(queries[0].reshape(GROUP, HEAD), tokens_of(0, range(CHUNKS)), 0)
        for k in range(CHUNKS):
            rows = slice(k * CHUNK, (k + 1) * CHUNK)
            own_o[k] = total[rows]
            own_m[k] = jnp.broadcast_to(top[rows], (CHUNK, HEAD))

    def give_back(k, i, total, top):
        part_o[k, i] = total[:, 0:HEAD].astype(BF16)
        part_s[k, i, 0:4, :] = jnp.transpose(jnp.broadcast_to(top, (CHUNK, HEAD)))[0:4, :]
        part_s[k, i, 4:8, :] = jnp.transpose(total[:, HEAD : 2 * HEAD])[0:4, :]
        back = device((-3, 3)[i], 0, 0)
        send(part_o.at[k, i], part_o_in.at[k, i], p_send.at[k, i, 0], p_recv.at[k, i, 0], back)
        send(part_s.at[k, i], part_s_in.at[k, i], p_send.at[k, i, 1], p_recv.at[k, i, 1], back)

    def attend_early():
        for i, (source, first) in enumerate(((1, 0), (2, 1))):
            for k in range(2):
                arrive(queries.at[source, k], q_recv.at[k, i])
            query = queries[source, 0:2].reshape(2 * CHUNK, HEAD)
            total, top = attend(query, tokens_of(source, range(2)), first)
            for k in range(2):
                rows = slice(k * CHUNK, (k + 1) * CHUNK)
                give_back(k, i, total[rows], top[rows])

    def attend_last():
        arrive(queries.at[1, 2], q_recv.at[2, 0])
        arrive(queries.at[2, 2], q_recv.at[2, 1])
        below, above = tokens_of(1, (2,)), tokens_of(2, (2,))
        total, top = over(queries[1, 2], below, 0, None, None)
        query = jnp.concatenate([queries[1, 2], queries[2, 2]], axis=0)
        query_token = jnp.concatenate([below, above], axis=0)
        state = (
            jnp.concatenate([total, jnp.zeros((CHUNK, 2 * HEAD), F32)], axis=0),
            jnp.concatenate([top, jnp.full((CHUNK, 1), NEG, F32)], axis=0),
        )
        total, top = lax.fori_loop(1, 3, lambda s, c: over(query, query_token, s, *c), state)
        give_back(2, 0, total[0:CHUNK], top[0:CHUNK])
        give_back(2, 1, total[CHUNK : 2 * CHUNK], top[CHUNK : 2 * CHUNK])

    def combine(k):
        total, low, top = own_o[k][:, 0:HEAD], own_o[k][:, HEAD : 2 * HEAD], own_m[k]
        for i in range(2):
            arrive(part_o_in.at[k, i], p_recv.at[k, i, 0])
            arrive(part_s_in.at[k, i], p_recv.at[k, i, 1])
            their_top = jnp.transpose(jnp.broadcast_to(part_s_in[k, i, 0:1, :], (CHUNK, HEAD)))
            their_low = jnp.transpose(jnp.broadcast_to(part_s_in[k, i, 4:5, :], (CHUNK, HEAD)))
            new_top = jnp.maximum(top, their_top)
            mine, theirs = jnp.exp2(top - new_top), jnp.exp2(their_top - new_top)
            total = total * mine + part_o_in[k, i].astype(F32) * theirs
            low = low * mine + their_low * theirs
            top = new_top
        result = (total / low).astype(BF16)
        own_head[k] = result
        attended[k, :, slot_of(head_slot(core))] = result
        for i, (cc, to) in enumerate(gatherers):
            slot = head_slot(cc)
            send(own_head.at[k], attended.at[k, :, slot_of(slot)], t_send.at[k, i], t_recv.at[k, slot], to)

    gatherers = [(0, device(0, 0, s, 0)) for s in (2, 1, 3)] + [(1, device(0, s, 0, 1)) for s in (2, 1, 3)]
    gatherers += [(other, partner)]
    gather_at, sum_at = gather_place(core), x * other + y * core

    def send_o_weight():
        for i, (cc, to) in enumerate(gatherers):
            if i < 6:
                ahead = (2, 1, 3)[i % 3]
                place = lax.rem((y if cc == 0 else x) + ahead, 4)
            else:
                place = gather_place(cc)
            for q in range(4):
                remote(
                    ow_ref.at[:, columns(cc, q, place)],
                    o_mat.at[slot_of(head_slot(cc)), pl.ds(q * 256, 256)],
                    w_send.at[1 + i], o_recv.at[head_slot(cc)], to,
                ).start()

    def other_heads(do):
        for ahead in range(1, 4):
            for c in range(2):
                do(2 * lax.rem(gather_at + ahead, 4) + c)
        do(2 * gather_at + other)

    def o_weight_arrive():
        own = o_mat.at[slot_of(head_slot(core)), :]
        pltpu.make_async_copy(own, own, local_sems.at[5]).wait()
        other_heads(lambda slot: arrive(o_mat.at[slot_of(slot), :], o_recv.at[slot]))

    def along(ahead):
        return device(0, ahead * other, ahead * core)

    def stage_one(k):
        other_heads(lambda slot: arrive(attended.at[k, :, slot_of(slot)], t_recv.at[k, slot]))
        for ahead in (2, 1, 3, 0):
            target = pl.ds(pl.multiple_of(lax.rem(sum_at + ahead, 4) * 256, 256), 256)
            value = nn_dot(attended[k], o_mat[:, target])
            if ahead == 0:
                mid[k] = value
            else:
                at = (k, ahead - 1)
                one_out[at] = value.astype(BF16)
                send(one_out.at[at], one_in.at[at], one_send.at[at], one_recv.at[at], along(ahead))

    def finish(k):
        value = mid[k]
        for i in range(3):
            arrive(one_in.at[k, i], one_recv.at[k, i])
            value = value + one_in[k, i].astype(F32)
        result = value.astype(BF16)
        for i in range(SHARDS):
            at = i * SHARD + k * PIECE
            out_ref[at : at + PIECE, :] = result[i * PIECE : (i + 1) * PIECE, :]

    a_mid(1)
    a_last(0)
    span_forward()
    a_mid(2)
    load_qw.wait()
    arrive(q_mat.at[:, pl.ds(pl.multiple_of(other * HEAD, HEAD), HEAD)], w_recv.at[0])
    project(0)
    a_last(1)
    finish_queries(0)
    a_last(2)
    project(1)
    finish_queries(1)
    project(2)
    finish_queries(2)
    send_o_weight()
    neighbours_arrive()
    attend_early()
    attend_last()
    attend_own()
    combine(0)
    combine(1)
    combine(2)
    o_weight_arrive()
    stage_one(0)
    stage_one(1)
    stage_one(2)
    finish(0)
    finish(1)
    finish(2)

    for copy in sent:
        copy.wait_send()
    for i in range(7):
        piece = o_mat.at[slot_of(i), :]
        remote(piece, piece, w_send.at[1 + i], o_recv.at[i], partner).wait_send()


def local(
    hidden, norm_gain, q_weight, q_bias, key_weight, key_bias, value_weight, value_bias, o_weight,
    cached_key_rows, cached_value_rows, keep_blocks, kept_counts, span_start,
):
    steps = np.arange(HEAD // 2, dtype=np.float64)
    frequency = (1000000.0 ** (-2.0 * steps / HEAD)).astype(np.float32)
    frequency = np.concatenate([frequency, frequency])[None, :]

    vmem = pl.BlockSpec(memory_space=pltpu.VMEM)
    smem = pl.BlockSpec(memory_space=pltpu.SMEM)
    hbm = pl.BlockSpec(memory_space=pl.ANY)
    dma = pltpu.SemaphoreType.DMA
    scratch = [
        pltpu.VMEM((SHARD, WIDTH), BF16),
        pltpu.VMEM((SHARD, WIDTH), BF16),
        pltpu.VMEM((CHUNKS, 2, CHUNK, QUART), BF16),
        pltpu.VMEM((HALF, 2 * HEAD), BF16),
        pltpu.VMEM((WIDTH, 2 * HEAD), BF16),
        pltpu.VMEM((8 * HEAD, 1024), BF16),
        pltpu.VMEM((32, BLOCK, HEAD), BF16),
        pltpu.VMEM((32, BLOCK, HEAD), BF16),
        pltpu.VMEM((3, KEPT, HEAD), BF16),
        pltpu.VMEM((3, KEPT, 2 * HEAD), BF16),
        pltpu.VMEM((3, GROUP, HEAD), BF16),
        pltpu.VMEM((3, GROUP, 2 * HEAD), BF16),
        pltpu.VMEM((3, 1, KEPT), F32),
        pltpu.VMEM((CHUNKS, CHUNK, HEAD), F32),
        pltpu.VMEM((CHUNKS, CHUNK, HEAD), F32),
        pltpu.VMEM((CHUNKS, 2, CHUNK, HEAD), F32),
        pltpu.VMEM((CHUNKS, CHUNK, HEAD), F32),
        pltpu.VMEM((3, CHUNKS, CHUNK, HEAD), BF16),
        pltpu.VMEM((CHUNKS, 2, CHUNK, HEAD), BF16),
        pltpu.VMEM((CHUNKS, 2, 8, CHUNK), F32),
        pltpu.VMEM((CHUNKS, 2, CHUNK, HEAD), BF16),
        pltpu.VMEM((CHUNKS, 2, 8, CHUNK), F32),
        pltpu.VMEM((CHUNKS, CHUNK, 2 * HEAD), F32),
        pltpu.VMEM((CHUNKS, CHUNK, HEAD), F32),
        pltpu.VMEM((CHUNKS, CHUNK, HEAD), BF16),
        pltpu.VMEM((CHUNKS, CHUNK, 8 * HEAD), BF16),
        pltpu.VMEM((CHUNKS, 3, CHUNK, 256), BF16),
        pltpu.VMEM((CHUNKS, 3, CHUNK, 256), BF16),
        pltpu.VMEM((CHUNKS, CHUNK, 256), F32),
        dma((7,)),
        dma((CHUNKS, 14)), dma((CHUNKS, 2, SHARDS)),
        dma((8,)), dma((1,)), dma((8,)),
        dma((2, 2)), dma((2, 3)),
        dma((2, SHARDS)), dma((2, SHARDS)),
        dma((2, 2)), dma((2, 3)),
        dma((CHUNKS,)), dma((CHUNKS,)),
        dma((CHUNKS, 2)), dma((CHUNKS, 2)),
        dma((CHUNKS, 2, 2)), dma((CHUNKS, 2, 2)),
        dma((CHUNKS, 7)), dma((CHUNKS, 8)),
        dma((CHUNKS, 3)), dma((CHUNKS, 3)),
    ]
    return pl.pallas_call(
        kernel,
        out_shape=jax.ShapeDtypeStruct((GROUP, 256), BF16),
        in_specs=[hbm, vmem, hbm, vmem, hbm, vmem, hbm, vmem, hbm, hbm, hbm, smem, smem, smem, vmem],
        out_specs=vmem,
        scratch_shapes=scratch,
        compiler_params=pltpu.CompilerParams(
            collective_id=0, has_side_effects=True, vmem_limit_bytes=56 * 1024 * 1024
        ),
        name="attention_sublayer",
    )(
        hidden, norm_gain, q_weight, q_bias, key_weight, key_bias, value_weight, value_bias, o_weight,
        cached_key_rows.reshape(32, BLOCK, HEAD), cached_value_rows.reshape(32, BLOCK, HEAD),
        keep_blocks, kept_counts, span_start, jnp.asarray(frequency),
    )


def solution(mesh):
    in_specs = (
        P(("ctx", "row"), None),
        P(),
        P(None, ("head", "row")),
        P(("head", "row")),
        P(None, "head"),
        P("head"),
        P(None, "head"),
        P("head"),
        P(("head", "row"), None),
        P("ctx", "head"),
        P("ctx", "head"),
        P("ctx", None),
        P(),
        P(),
    )
    out_specs = P("ctx", ("head", "row"))
    return jax.shard_map(local, mesh=mesh, in_specs=in_specs, out_specs=out_specs, check_vma=False)
```

```python
import math

import jax
import jax.numpy as jnp
import numpy as np
from jax import lax
from jax.experimental import pallas as pl
from jax.experimental.pallas import tpu as pltpu
from jax.sharding import PartitionSpec as P

MESH = pl.DeviceIdType.MESH
F32 = jnp.float32
BF16 = jnp.bfloat16

N_CTX = 8
WIDTH = 8192
HALF = 4096
QUART = 2048
HEAD = 128
BLOCK = 128
KEEP = 8
SHARDS = 8
SHARD = 48
CHUNKS = 3
PIECE = 16
CHUNK = SHARDS * PIECE
GROUP = SHARDS * SHARD
KEPT = KEEP * BLOCK
NEG = -1e30
LOG2E = math.log2(math.e)


def nt_dot(a, b):
    return lax.dot_general(a, b, (((1,), (1,)), ((), ())), preferred_element_type=F32)


def nn_dot(a, b):
    return lax.dot_general(a, b, (((1,), (0,)), ((), ())), preferred_element_type=F32)


def kernel(
    hidden_hbm, gain_ref, qw_ref, qb_ref, kw_ref, kb_ref, vw_ref, vb_ref, ow_ref, ck_ref, cv_ref,
    blocks_ref, counts_ref, start_ref, freq_ref,
    out_ref,
    hidden_ref, normed, gathered, q_mat, kv_mat, o_mat, cache_k, cache_v,
    pre_k, pre_v, span_k, span_v, mask, cos_ref, sin_ref,
    halves, halves_in, queries, part_o, part_s, part_o_in, part_s_in,
    own_o, own_m, own_head, attended, one_out, one_in, mid,
    local_sems, a_send, a_recv, w_send, w_recv, o_recv, pre_send, pre_recv, row_send, row_recv, span_send, span_recv,
    h_send, h_recv, q_send, q_recv, p_send, p_recv, t_send, t_recv, one_send, one_recv,
):
    z = lax.axis_index("ctx")
    head = lax.axis_index("head")
    row = lax.axis_index("row")
    core = lax.rem(head, 2)
    x_lo = row // 4
    y = lax.rem(row, 4)
    x = 2 * (head // 2) + x_lo
    other = 1 - core

    def device(dz, dx, dy, dc=None):
        xx = lax.rem(x + dx + 4, 4)
        yy = lax.rem(y + dy + 4, 4)
        cc = core if dc is None else dc
        return (lax.rem(z + dz + 8, 8), 2 * (xx // 2) + cc, 4 * lax.rem(xx, 2) + yy)

    def row_peer(step):
        return (z, head, lax.rem(row + step, SHARDS))

    partner = (z, 2 * (head // 2) + other, row)

    def remote(src, dst, send, recv, to):
        return pltpu.make_async_remote_copy(
            src_ref=src, dst_ref=dst, send_sem=send, recv_sem=recv, device_id=to, device_id_type=MESH
        )

    barrier = pltpu.get_barrier_semaphore()
    partners = [partner]
    partners += [device(0, s, 0, c) for s in range(1, 4) for c in range(2)]
    partners += [device(0, 0, s, c) for s in range(1, 4) for c in range(2)]
    beside = 4 * (1 - x_lo)
    partners += [(z, head, beside + lax.rem(y + s, 4)) for s in range(1, 4)]
    partners += [device(dz, 0, 0) for dz in (1, -1, 3, -3)]
    for to in partners:
        pl.semaphore_signal(barrier, inc=1, device_id=to, device_id_type=MESH)

    sent = []

    def send(src, dst, send_sem, recv_sem, to):
        copy = remote(src, dst, send_sem, recv_sem, to)
        copy.start()
        sent.append(copy)

    def arrive(dst, recv_sem):
        remote(dst, dst, recv_sem, recv_sem, partner).wait_recv()

    def load(src, dst, i):
        copy = pltpu.make_async_copy(src, dst, local_sems.at[i])
        copy.start()
        return copy

    load_hidden = load(hidden_hbm, hidden_ref, 6)
    load_k = load(ck_ref, cache_k, 0)
    load_v = load(cv_ref, cache_v, 1)
    load_kw = load(kw_ref, kv_mat.at[:, 0:HEAD], 2)
    load_vw = load(vw_ref, kv_mat.at[:, HEAD : 2 * HEAD], 3)
    own_cols = pl.ds(pl.multiple_of(core * HEAD, HEAD), HEAD)
    load_qw = load(qw_ref.at[pl.ds(pl.multiple_of(core * HALF, HALF), HALF), :], q_mat.at[:, own_cols], 4)

    def gather_place(cc):
        return y * (1 - cc) + x * cc

    def columns(cc, summed, place):
        xx = summed * (1 - cc) + place * cc
        yy = place * (1 - cc) + summed * cc
        return pl.ds(pl.multiple_of((2 * (xx // 2) + cc) * 2048 + (4 * lax.rem(xx, 2) + yy) * 256, 256), 256)

    def head_slot(cc):
        return 2 * gather_place(cc) + core

    def slot_of(index):
        return pl.ds(pl.multiple_of(index * HEAD, HEAD), HEAD)

    for q in range(4):
        pltpu.make_async_copy(
            ow_ref.at[:, columns(core, q, gather_place(core))],
            o_mat.at[slot_of(head_slot(core)), pl.ds(q * 256, 256)],
            local_sems.at[5],
        ).start()

    def rows_of(shard):
        return pl.ds(pl.multiple_of(shard * PIECE, PIECE), PIECE)

    def normalise(k):
        rows = slice(k * PIECE, (k + 1) * PIECE)
        total = jnp.zeros((PIECE, 1), F32)
        for i in range(8):
            part = hidden_ref[rows, i * 1024 : (i + 1) * 1024].astype(F32)
            total = total + jnp.sum(part * part, axis=1, keepdims=True)
        factor = lax.rsqrt(total / WIDTH + 1e-6)
        for i in range(8):
            cols = slice(i * 1024, (i + 1) * 1024)
            part = hidden_ref[rows, cols].astype(F32) * factor * gain_ref[cols].astype(F32).reshape(1, 1024)
            normed[rows, cols] = part.astype(BF16)
        for f in range(2):
            cols = pl.ds(pl.multiple_of(core * HALF + f * QUART, QUART), QUART)
            gathered[k, f, rows_of(row), :] = normed[rows, cols]

    y_up, y_down = device(0, 0, 1), device(0, 0, -1)
    x_up, x_down = device(0, 1, 0), device(0, -1, 0)
    a_count = [0, 0, 0]

    def forward(k, f, shard, to):
        piece = gathered.at[k, f, rows_of(shard), :]
        send(piece, piece, a_send.at[k, a_count[k]], a_recv.at[k, f, shard], to)
        a_count[k] += 1

    def shard_at(dy, flip=False):
        xl = 1 - x_lo if flip else x_lo
        return 4 * xl + lax.rem(y + dy + 4, 4)

    def a_arrive(k, f, shard):
        arrive(gathered.at[k, f, rows_of(shard), :], a_recv.at[k, f, shard])

    def a_start(k):
        forward(k, 0, row, x_up)
        forward(k, 0, row, y_up)
        forward(k, 1, row, x_down)
        forward(k, 1, row, y_down)
        forward(k, 1, row, y_up)
        forward(k, 0, row, y_down)

    def a_mid(k):
        below, above = shard_at(-1), shard_at(1)
        a_arrive(k, 0, below)
        forward(k, 0, below, y_up)
        forward(k, 0, below, x_up)
        a_arrive(k, 1, above)
        forward(k, 1, above, y_down)
        forward(k, 1, above, x_down)
        a_arrive(k, 1, below)
        forward(k, 1, below, x_down)
        a_arrive(k, 0, above)
        forward(k, 0, above, x_up)

    def a_last(k):
        far = shard_at(2)
        a_arrive(k, 0, far)
        forward(k, 0, far, x_up)
        a_arrive(k, 1, far)
        forward(k, 1, far, x_down)

    load_hidden.wait()
    normalise(0)
    normalise(1)
    normalise(2)
    pl.semaphore_wait(barrier, len(partners))
    a_start(0)
    a_start(1)

    send(
        qw_ref.at[pl.ds(pl.multiple_of(other * HALF, HALF), HALF), :],
        q_mat.at[:, own_cols], w_send.at[0], w_recv.at[0], partner,
    )
    load_k.wait()
    load_v.wait()
    for j in range(KEEP):
        pre_k[1, j * BLOCK : (j + 1) * BLOCK, :] = cache_k[blocks_ref[0, j]]
        pre_v[1, j * BLOCK : (j + 1) * BLOCK, 0:HEAD] = cache_v[blocks_ref[0, j]]
    z_up, z_down = device(1, 0, 0), device(-1, 0, 0)
    left = pl.ds(0, HEAD)
    for s in range(3):
        pre_v[s, :, HEAD : 2 * HEAD] = jnp.ones((KEPT, HEAD), BF16)
        span_v[s, :, HEAD : 2 * HEAD] = jnp.ones((GROUP, HEAD), BF16)
        live = counts_ref[lax.rem(z + s + 7, N_CTX)]
        slot_index = lax.broadcasted_iota(jnp.int32, (1, KEPT), 1) // BLOCK
        mask[s] = jnp.where(slot_index < live, 0.0, NEG).astype(F32)

    token = lax.broadcasted_iota(jnp.int32, (CHUNK, 1), 0)
    token = (token // PIECE) * SHARD + lax.rem(token, PIECE)
    sign = jnp.where(lax.broadcasted_iota(jnp.int32, (1, HEAD), 1) < HEAD // 2, -1.0, 1.0)

    def angles_of(k):
        positions = (start_ref[0] + z * GROUP + k * PIECE + token).astype(F32)
        angles = positions * freq_ref[...]
        cos_ref[k] = jnp.cos(angles)
        sin_ref[k] = jnp.sin(angles) * sign

    for k in range(CHUNKS):
        angles_of(k)

    def rotated(values, cosine, sine):
        return values * cosine + pltpu.roll(values, HEAD // 2, 1) * sine

    load_kw.wait()
    load_vw.wait()

    def kv_step(i, total):
        at = pl.ds(pl.multiple_of(i * 1024, 1024), 1024)
        return total + nn_dot(normed[:, at], kv_mat[at, :])

    def span_rows(shard):
        return pl.ds(pl.multiple_of(shard * SHARD, SHARD), SHARD)

    pair = lax.fori_loop(0, 4, kv_step, jnp.zeros((SHARD, 2 * HEAD), F32))
    a_mid(0)
    a_start(2)
    for i, (slot, to) in enumerate(((0, z_up), (2, z_down))):
        send(pre_k.at[1], pre_k.at[slot], pre_send.at[0, i], pre_recv.at[0, slot], to)
        send(pre_v.at[1, :, left], pre_v.at[slot, :, left], pre_send.at[1, i], pre_recv.at[1, slot], to)

    pair = lax.fori_loop(4, 8, kv_step, pair)
    key_part = pair[:, 0:HEAD] + kb_ref[...].astype(F32).reshape(1, HEAD)
    value_part = pair[:, HEAD : 2 * HEAD] + vb_ref[...].astype(F32).reshape(1, HEAD)
    own_cos = jnp.concatenate([cos_ref[k, rows_of(row), :] for k in range(CHUNKS)], axis=0)
    own_sin = jnp.concatenate([sin_ref[k, rows_of(row), :] for k in range(CHUNKS)], axis=0)

    span_k[1, span_rows(row), :] = rotated(key_part, own_cos, own_sin).astype(BF16)
    span_v[1, span_rows(row), 0:HEAD] = value_part.astype(BF16)
    for s in range(1, SHARDS):
        here = span_k.at[1, span_rows(row), :]
        send(here, here, row_send.at[0, s], row_recv.at[0, row], row_peer(s))
        here = span_v.at[1, span_rows(row), left]
        send(here, here, row_send.at[1, s], row_recv.at[1, row], row_peer(s))

    def span_forward():
        for s in range(1, SHARDS):
            peer = lax.rem(row + s, SHARDS)
            arrive(span_k.at[1, span_rows(peer), :], row_recv.at[0, peer])
            arrive(span_v.at[1, span_rows(peer), left], row_recv.at[1, peer])
        for i, (slot, to) in enumerate(((0, z_up), (2, z_down))):
            send(span_k.at[1], span_k.at[slot], span_send.at[0, i], span_recv.at[0, slot], to)
            send(span_v.at[1, :, left], span_v.at[slot, :, left], span_send.at[1, i], span_recv.at[1, slot], to)

    def neighbours_arrive():
        for slot in (0, 2):
            arrive(pre_k.at[slot], pre_recv.at[0, slot])
            arrive(pre_v.at[slot, :, left], pre_recv.at[1, slot])
            arrive(span_k.at[slot], span_recv.at[0, slot])
            arrive(span_v.at[slot, :, left], span_recv.at[1, slot])

    def project(k):
        for shard_dy in range(4):
            for f in range(2):
                a_arrive(k, f, shard_at(shard_dy, True))
        both = nn_dot(gathered[k, 0], q_mat[0:QUART, :]) + nn_dot(gathered[k, 1], q_mat[QUART:HALF, :])
        halves[k, 0] = both[:, 0:HEAD]
        halves[k, 1] = both[:, HEAD : 2 * HEAD]
        send(halves.at[k, other], halves_in.at[k], h_send.at[k], h_recv.at[k], partner)

    def finish_queries(k):
        arrive(halves_in.at[k], h_recv.at[k])
        values = halves[k, core] + halves_in[k] + qb_ref[...].astype(F32).reshape(1, HEAD)
        values = rotated(values, cos_ref[k], sin_ref[k]) * (LOG2E / math.sqrt(HEAD))
        queries[0, k] = values.astype(BF16)
        send(queries.at[0, k], queries.at[1, k], q_send.at[k, 0], q_recv.at[k, 0], device(3, 0, 0))
        send(queries.at[0, k], queries.at[2, k], q_send.at[k, 1], q_recv.at[k, 1], device(-3, 0, 0))

    key_token = lax.broadcasted_iota(jnp.int32, (1, GROUP), 1)

    def tokens_of(source, chunks):
        group = lax.rem(z + (0, 5, 3)[source], N_CTX)
        return jnp.concatenate([group * GROUP + k * PIECE + token for k in chunks], axis=0)

    def over(query, query_token, slot, total, top):
        prefix = nt_dot(query, pre_k[slot]) + mask[slot]
        span = nt_dot(query, span_k[slot])
        key_group = lax.rem(z + slot + 7, N_CTX)
        span = jnp.where(key_group * GROUP + key_token <= query_token, span, NEG)
        new_top = jnp.maximum(jnp.max(prefix, axis=1, keepdims=True), jnp.max(span, axis=1, keepdims=True))
        if top is not None:
            new_top = jnp.maximum(new_top, top)
        blended = nn_dot(jnp.exp2(prefix - new_top).astype(BF16), pre_v[slot])
        blended = blended + nn_dot(jnp.exp2(span - new_top).astype(BF16), span_v[slot])
        if top is not None:
            blended = blended + total * jnp.exp2(top - new_top)
        return blended, new_top

    def attend(query, query_token, first):
        state = over(query, query_token, first, None, None)
        return lax.fori_loop(first + 1, 3, lambda s, c: over(query, query_token, s, *c), state)

    def attend_own():
        total, top = attend(queries[0].reshape(GROUP, HEAD), tokens_of(0, range(CHUNKS)), 0)
        for k in range(CHUNKS):
            rows = slice(k * CHUNK, (k + 1) * CHUNK)
            own_o[k] = total[rows]
            own_m[k] = jnp.broadcast_to(top[rows], (CHUNK, HEAD))

    def give_back(k, i, total, top):
        part_o[k, i] = total[:, 0:HEAD].astype(BF16)
        part_s[k, i, 0:4, :] = jnp.transpose(jnp.broadcast_to(top, (CHUNK, HEAD)))[0:4, :]
        part_s[k, i, 4:8, :] = jnp.transpose(total[:, HEAD : 2 * HEAD])[0:4, :]
        back = device((-3, 3)[i], 0, 0)
        send(part_o.at[k, i], part_o_in.at[k, i], p_send.at[k, i, 0], p_recv.at[k, i, 0], back)
        send(part_s.at[k, i], part_s_in.at[k, i], p_send.at[k, i, 1], p_recv.at[k, i, 1], back)

    def attend_sources(begin, end):
        chunks = range(begin, end)
        rows = (end - begin) * CHUNK
        for i in range(2):
            for k in chunks:
                arrive(queries.at[1 + i, k], q_recv.at[k, i])
        below, above = tokens_of(1, chunks), tokens_of(2, chunks)
        lower = queries[1, begin:end].reshape(rows, HEAD)
        upper = queries[2, begin:end].reshape(rows, HEAD)
        total, top = over(lower, below, 0, None, None)
        query = jnp.concatenate([lower, upper], axis=0)
        query_token = jnp.concatenate([below, above], axis=0)
        state = (
            jnp.concatenate([total, jnp.zeros((rows, 2 * HEAD), F32)], axis=0),
            jnp.concatenate([top, jnp.full((rows, 1), NEG, F32)], axis=0),
        )
        total, top = lax.fori_loop(1, 3, lambda s, c: over(query, query_token, s, *c), state)
        for i in range(2):
            for k in chunks:
                at = i * rows + (k - begin) * CHUNK
                give_back(k, i, total[at : at + CHUNK], top[at : at + CHUNK])

    def combine(k):
        total, low, top = own_o[k][:, 0:HEAD], own_o[k][:, HEAD : 2 * HEAD], own_m[k]
        for i in range(2):
            arrive(part_o_in.at[k, i], p_recv.at[k, i, 0])
            arrive(part_s_in.at[k, i], p_recv.at[k, i, 1])
            their_top = jnp.transpose(jnp.broadcast_to(part_s_in[k, i, 0:1, :], (CHUNK, HEAD)))
            their_low = jnp.transpose(jnp.broadcast_to(part_s_in[k, i, 4:5, :], (CHUNK, HEAD)))
            new_top = jnp.maximum(top, their_top)
            mine, theirs = jnp.exp2(top - new_top), jnp.exp2(their_top - new_top)
            total = total * mine + part_o_in[k, i].astype(F32) * theirs
            low = low * mine + their_low * theirs
            top = new_top
        result = (total / low).astype(BF16)
        own_head[k] = result
        attended[k, :, slot_of(head_slot(core))] = result
        for i, (cc, to) in enumerate(gatherers):
            slot = head_slot(cc)
            send(own_head.at[k], attended.at[k, :, slot_of(slot)], t_send.at[k, i], t_recv.at[k, slot], to)

    gatherers = [(0, device(0, 0, s, 0)) for s in (2, 1, 3)] + [(1, device(0, s, 0, 1)) for s in (2, 1, 3)]
    gatherers += [(other, partner)]
    gather_at, sum_at = gather_place(core), x * other + y * core

    def send_o_weight():
        for i, (cc, to) in enumerate(gatherers):
            if i < 6:
                ahead = (2, 1, 3)[i % 3]
                place = lax.rem((y if cc == 0 else x) + ahead, 4)
            else:
                place = gather_place(cc)
            for q in range(4):
                remote(
                    ow_ref.at[:, columns(cc, q, place)],
                    o_mat.at[slot_of(head_slot(cc)), pl.ds(q * 256, 256)],
                    w_send.at[1 + i], o_recv.at[head_slot(cc)], to,
                ).start()

    def other_heads(do):
        for ahead in range(1, 4):
            for c in range(2):
                do(2 * lax.rem(gather_at + ahead, 4) + c)
        do(2 * gather_at + other)

    def o_weight_arrive():
        own = o_mat.at[slot_of(head_slot(core)), :]
        pltpu.make_async_copy(own, own, local_sems.at[5]).wait()
        other_heads(lambda slot: arrive(o_mat.at[slot_of(slot), :], o_recv.at[slot]))

    def along(ahead):
        return device(0, ahead * other, ahead * core)

    def stage_one(k):
        other_heads(lambda slot: arrive(attended.at[k, :, slot_of(slot)], t_recv.at[k, slot]))
        for ahead in (2, 1, 3, 0):
            target = pl.ds(pl.multiple_of(lax.rem(sum_at + ahead, 4) * 256, 256), 256)
            value = nn_dot(attended[k], o_mat[:, target])
            if ahead == 0:
                mid[k] = value
            else:
                at = (k, ahead - 1)
                one_out[at] = value.astype(BF16)
                send(one_out.at[at], one_in.at[at], one_send.at[at], one_recv.at[at], along(ahead))

    def finish(k):
        value = mid[k]
        for i in range(3):
            arrive(one_in.at[k, i], one_recv.at[k, i])
            value = value + one_in[k, i].astype(F32)
        result = value.astype(BF16)
        for i in range(SHARDS):
            at = i * SHARD + k * PIECE
            out_ref[at : at + PIECE, :] = result[i * PIECE : (i + 1) * PIECE, :]

    a_mid(1)
    a_last(0)
    span_forward()
    a_mid(2)
    load_qw.wait()
    arrive(q_mat.at[:, pl.ds(pl.multiple_of(other * HEAD, HEAD), HEAD)], w_recv.at[0])
    project(0)
    a_last(1)
    finish_queries(0)
    a_last(2)
    project(1)
    finish_queries(1)
    project(2)
    finish_queries(2)
    send_o_weight()
    neighbours_arrive()
    attend_sources(0, 2)
    attend_sources(2, 3)
    attend_own()
    combine(0)
    combine(1)
    combine(2)
    o_weight_arrive()
    stage_one(0)
    stage_one(1)
    stage_one(2)
    finish(0)
    finish(1)
    finish(2)

    for copy in sent:
        copy.wait_send()
    for i in range(7):
        piece = o_mat.at[slot_of(i), :]
        remote(piece, piece, w_send.at[1 + i], o_recv.at[i], partner).wait_send()


def local(
    hidden, norm_gain, q_weight, q_bias, key_weight, key_bias, value_weight, value_bias, o_weight,
    cached_key_rows, cached_value_rows, keep_blocks, kept_counts, span_start,
):
    steps = np.arange(HEAD // 2, dtype=np.float64)
    frequency = (1000000.0 ** (-2.0 * steps / HEAD)).astype(np.float32)
    frequency = np.concatenate([frequency, frequency])[None, :]

    vmem = pl.BlockSpec(memory_space=pltpu.VMEM)
    smem = pl.BlockSpec(memory_space=pltpu.SMEM)
    hbm = pl.BlockSpec(memory_space=pl.ANY)
    dma = pltpu.SemaphoreType.DMA
    scratch = [
        pltpu.VMEM((SHARD, WIDTH), BF16),
        pltpu.VMEM((SHARD, WIDTH), BF16),
        pltpu.VMEM((CHUNKS, 2, CHUNK, QUART), BF16),
        pltpu.VMEM((HALF, 2 * HEAD), BF16),
        pltpu.VMEM((WIDTH, 2 * HEAD), BF16),
        pltpu.VMEM((8 * HEAD, 1024), BF16),
        pltpu.VMEM((32, BLOCK, HEAD), BF16),
        pltpu.VMEM((32, BLOCK, HEAD), BF16),
        pltpu.VMEM((3, KEPT, HEAD), BF16),
        pltpu.VMEM((3, KEPT, 2 * HEAD), BF16),
        pltpu.VMEM((3, GROUP, HEAD), BF16),
        pltpu.VMEM((3, GROUP, 2 * HEAD), BF16),
        pltpu.VMEM((3, 1, KEPT), F32),
        pltpu.VMEM((CHUNKS, CHUNK, HEAD), F32),
        pltpu.VMEM((CHUNKS, CHUNK, HEAD), F32),
        pltpu.VMEM((CHUNKS, 2, CHUNK, HEAD), F32),
        pltpu.VMEM((CHUNKS, CHUNK, HEAD), F32),
        pltpu.VMEM((3, CHUNKS, CHUNK, HEAD), BF16),
        pltpu.VMEM((CHUNKS, 2, CHUNK, HEAD), BF16),
        pltpu.VMEM((CHUNKS, 2, 8, CHUNK), F32),
        pltpu.VMEM((CHUNKS, 2, CHUNK, HEAD), BF16),
        pltpu.VMEM((CHUNKS, 2, 8, CHUNK), F32),
        pltpu.VMEM((CHUNKS, CHUNK, 2 * HEAD), F32),
        pltpu.VMEM((CHUNKS, CHUNK, HEAD), F32),
        pltpu.VMEM((CHUNKS, CHUNK, HEAD), BF16),
        pltpu.VMEM((CHUNKS, CHUNK, 8 * HEAD), BF16),
        pltpu.VMEM((CHUNKS, 3, CHUNK, 256), BF16),
        pltpu.VMEM((CHUNKS, 3, CHUNK, 256), BF16),
        pltpu.VMEM((CHUNKS, CHUNK, 256), F32),
        dma((7,)),
        dma((CHUNKS, 14)), dma((CHUNKS, 2, SHARDS)),
        dma((8,)), dma((1,)), dma((8,)),
        dma((2, 2)), dma((2, 3)),
        dma((2, SHARDS)), dma((2, SHARDS)),
        dma((2, 2)), dma((2, 3)),
        dma((CHUNKS,)), dma((CHUNKS,)),
        dma((CHUNKS, 2)), dma((CHUNKS, 2)),
        dma((CHUNKS, 2, 2)), dma((CHUNKS, 2, 2)),
        dma((CHUNKS, 7)), dma((CHUNKS, 8)),
        dma((CHUNKS, 3)), dma((CHUNKS, 3)),
    ]
    return pl.pallas_call(
        kernel,
        out_shape=jax.ShapeDtypeStruct((GROUP, 256), BF16),
        in_specs=[hbm, vmem, hbm, vmem, hbm, vmem, hbm, vmem, hbm, hbm, hbm, smem, smem, smem, vmem],
        out_specs=vmem,
        scratch_shapes=scratch,
        compiler_params=pltpu.CompilerParams(
            collective_id=0, has_side_effects=True, vmem_limit_bytes=56 * 1024 * 1024
        ),
        name="attention_sublayer",
    )(
        hidden, norm_gain, q_weight, q_bias, key_weight, key_bias, value_weight, value_bias, o_weight,
        cached_key_rows.reshape(32, BLOCK, HEAD), cached_value_rows.reshape(32, BLOCK, HEAD),
        keep_blocks, kept_counts, span_start, jnp.asarray(frequency),
    )


def solution(mesh):
    in_specs = (
        P(("ctx", "row"), None),
        P(),
        P(None, ("head", "row")),
        P(("head", "row")),
        P(None, "head"),
        P("head"),
        P(None, "head"),
        P("head"),
        P(("head", "row"), None),
        P("ctx", "head"),
        P("ctx", "head"),
        P("ctx", None),
        P(),
        P(),
    )
    out_specs = P("ctx", ("head", "row"))
    return jax.shard_map(local, mesh=mesh, in_specs=in_specs, out_specs=out_specs, check_vma=False)
```
